128 devices in a mesh: dom: 32 (over z, y, core), rep: 4 (over x).
Axes of the slice: x: 4, y: 4, z: 4, core: 2. Of those that a mesh axis runs over, the one named last changes fastest.
Arguments:
- own_values: bfloat16 [32768, 1024], P('dom'), may hold values from -6 to 6
- own_scale: bfloat16 [256], P('dom'), may hold values from 0.25 to 4
- halo_cache: bfloat16 [131072, 1024], P('dom'), may hold values from -6 to 6
- send_list: int32 [32, 32], P('dom'), may hold values from 0 to 7
- batch_ids: int32 [32, 64], P('dom', 'rep'), may hold values from 0 to 7
- neighbor_blocks: int32 [32, 64, 6], P('dom', 'rep'), may hold values from 0 to 39, as said below
- edge_tiles: bfloat16 [32, 64, 6, 128, 128], P('dom', 'rep'), may hold values from -0.21875 to 0.21875
- w_self: bfloat16 [1024, 1024], replicated, may hold values from -0.1875 to 0.1875
- w_neigh: bfloat16 [1024, 1024], replicated, may hold values from -0.1875 to 0.1875
- cotangent: bfloat16 [262144, 1024], P(('dom', 'rep')), may hold values from -6 to 6
Outputs:
- output_rows: bfloat16 [262144, 1024], P(('dom', 'rep'))
- grad_weights: float32 [2048, 1024], P(('dom', 'rep'))
The draws below stay inside these ranges and needn't reach their ends.
Inputs may be any that keep to these rules, and one draw needn't show every extreme that they name: `neighbor_blocks`: entries below 8 name a partition's own blocks, 8 + p names the block received from partition p; the rows of each device name every one of the 32 received blocks, and block 0 at least once.
All inputs are finite; a program needn't handle non-finite values.
Results may differ from the reference program's by a relative error of at most 0.014.
Values may be sent and summed in bfloat16 or wider, within the bound.
A program may use at most 192 MiB of HBM per device.

```python
import math
import jax
import jax.numpy as jnp
from jax import lax

D = 1024
BLOCK = 128
K = 6
LB = 8
TBD = 16
TARGETS = 262144
N_DOM = 32
N_REP = 4


def draw_neighbor_blocks(key, part):
    key = jax.random.fold_in(key, 11)

    def draw_device(subkey):
        key_fill, key_halo, key_shuffle = jax.random.split(subkey, 3)
        total_slots = TBD * K
        filler = jax.random.randint(key_fill, (total_slots,), 0, LB + N_DOM)
        halo_slots = jax.random.permutation(key_halo, N_DOM) + LB
        filler = filler.at[:N_DOM].set(halo_slots)
        filler = filler.at[N_DOM].set(0)
        shuffle = jax.random.permutation(key_shuffle, total_slots)
        return filler[shuffle].reshape(TBD, K)
    device_keys = jax.random.split(key, N_DOM * N_REP)
    blocks = jax.vmap(draw_device)(device_keys)
    return blocks.reshape(N_DOM, N_REP * TBD, K).astype(jnp.int32)


def plant(drawn, key, low, top_value):
    shape = drawn.shape
    spot = [jax.random.randint(jax.random.fold_in(key, axis), (), 0, shape[axis]) for axis in range(len(shape))]
    drawn = drawn.at[tuple(spot)].set(low)
    longest = shape.index(max(shape))
    spot[longest] = (spot[longest] + 1) % shape[longest]
    return drawn.at[tuple(spot)].set(top_value)


def level_of(own_key, dims, pieces, smallest, top_value):
    level, own = 1.0, jax.random.fold_in(own_key, 6)
    for dim, parts in pieces:
        heights = jnp.exp(jax.random.uniform(jax.random.fold_in(own, dim), (parts,), jnp.float32, smallest / len(pieces), top_value / len(pieces)))
        level = level * jnp.repeat(heights, dims[dim] // parts).reshape([-1 if axis == dim else 1 for axis in range(len(dims))])
    return level


def noise(own_key, shape, width, bound, pieces=(), kind=jnp.bfloat16):
    gain = level_of(own_key, shape, pieces, -0.22, 0.18) if pieces else 1.0
    drawn = jax.random.normal(own_key, shape, jnp.float32) * width * gain
    return jnp.minimum(jnp.maximum(drawn, -bound), bound).astype(kind)


def setup_inputs(seed: int = 0) -> dict:
    key_list = jax.random.split(jax.random.key(seed), 11)
    own_values = noise(key_list[0], (N_DOM * LB * BLOCK, D), 1.0, 6.0, ((0, 32),))
    own_scale = jnp.clip(jnp.exp(math.log(4.0) - 2.7725887 * jax.random.uniform(key_list[1], (N_DOM * LB,), jnp.float32) ** level_of(key_list[1], (N_DOM * LB,), ((0, 32),), -0.2, 0.2)), 0.25, 4.0).astype(jnp.bfloat16)
    halo_cache = noise(key_list[2], (N_DOM * N_DOM * BLOCK, D), 1.0, 6.0, ((0, 32),))
    send_list = plant(jax.random.randint(key_list[3], (N_DOM, N_DOM), 0, LB), jax.random.fold_in(key_list[3], 1), 0, LB - 1).astype(jnp.int32)
    batch_ids = plant(jax.random.randint(key_list[4], (N_DOM, N_REP * TBD), 0, LB), jax.random.fold_in(key_list[4], 1), 0, LB - 1).astype(jnp.int32)
    neighbor_blocks = draw_neighbor_blocks(jax.random.fold_in(key_list[10], 71), 0)
    edge_tiles = noise(key_list[6], (N_DOM, N_REP * TBD, K, BLOCK, BLOCK), (K * BLOCK) ** -0.5, 0.21875, ((0, 32), (1, 4)))
    w_self = noise(key_list[7], (D, D), D ** -0.5, 0.1875)
    w_neigh = noise(key_list[8], (D, D), D ** -0.5, 0.1875)
    cotangent = noise(key_list[9], (TARGETS, D), 1.0, 6.0, ((0, 128),))
    return dict(own_values=own_values, own_scale=own_scale, halo_cache=halo_cache, send_list=send_list, batch_ids=batch_ids, neighbor_blocks=neighbor_blocks, edge_tiles=edge_tiles, w_self=w_self, w_neigh=w_neigh, cotangent=cotangent)


MOMENTUM = 0.6

def reference(own_values, own_scale, halo_cache, send_list, batch_ids, neighbor_blocks, edge_tiles, w_self, w_neigh, cotangent):
    feat_width = own_values.shape[1]
    own_blocks = own_values.reshape(N_DOM, LB, BLOCK, feat_width)
    scales = own_scale.reshape(N_DOM, LB).astype(jnp.float32)
    own_deq = (own_blocks.astype(jnp.float32) * scales[:, :, None, None]).astype(jnp.bfloat16)
    caches = halo_cache.reshape(N_DOM, N_DOM, BLOCK, feat_width)
    cot_parts = cotangent.reshape(N_DOM, N_REP * TBD * BLOCK, feat_width)
    sources = jnp.arange(N_DOM, dtype=jnp.int32)

    def per_part(grad_total, part_index):
        chosen = send_list[:, part_index].astype(jnp.int32)
        fresh_rows = own_blocks[sources, chosen].astype(jnp.float32) * scales[sources, chosen][:, None, None]
        halo_rows = (MOMENTUM * fresh_rows + (1.0 - MOMENTUM) * caches[part_index].astype(jnp.float32)).astype(jnp.bfloat16)
        lookup = jnp.concatenate([own_deq[part_index], halo_rows], axis=0)
        gathered = lookup[neighbor_blocks[part_index]]
        summed = jnp.einsum('tkij,tkjd->tid', edge_tiles[part_index].astype(jnp.float32), gathered.astype(jnp.float32)).astype(jnp.bfloat16)
        self_rows = own_deq[part_index][batch_ids[part_index]]
        self_flat = self_rows.reshape(-1, feat_width)
        summed_flat = summed.reshape(-1, feat_width)
        pre_act = jnp.dot(self_flat, w_self, preferred_element_type=jnp.float32) + jnp.dot(summed_flat, w_neigh, preferred_element_type=jnp.float32)
        sigmoid_z = jax.nn.sigmoid(pre_act)
        out_part = (pre_act * sigmoid_z).astype(jnp.bfloat16)
        delta = (cot_parts[part_index].astype(jnp.float32) * sigmoid_z * (1.0 + pre_act * (1.0 - sigmoid_z))).astype(jnp.bfloat16)
        stacked = jnp.concatenate([self_flat, summed_flat], axis=1)
        term = lax.dot_general(stacked, delta, (((0,), (0,)), ((), ())), preferred_element_type=jnp.float32)
        return (grad_total + term, out_part)
    start_grad = jnp.zeros((2 * feat_width, feat_width), jnp.float32)
    grad_total, outputs = lax.scan(per_part, start_grad, jnp.arange(N_DOM, dtype=jnp.int32))
    return (outputs.reshape(-1, feat_width), grad_total * (1.0 / math.sqrt(TARGETS)))
```

```python
import functools
import math

import jax
import jax.numpy as jnp
from jax import lax
from jax.experimental import pallas as pl
from jax.experimental.pallas import tpu as pltpu
from jax.sharding import PartitionSpec as P

MOMENTUM = 0.6
MESH = pl.DeviceIdType.MESH
BLOCK = 128
FEATS = 1024
PHASES = 4
WIDE = FEATS // PHASES
SLOTS = 16
SUBS = 8
LANES = FEATS // SUBS
F32 = jnp.float32
BF16 = jnp.bfloat16


def place():
    dom = lax.axis_index("dom")
    return dom // 8, lax.rem(dom // 2, 4), lax.rem(dom, 2), lax.axis_index("rep")


def dom_of(z, y, c):
    return (z * 4 + y) * 2 + c


def halo_kernel(
    send_ref, scale_ref, near_ref, own_ref, edge_ref, cache_hbm,
    summed_ref,
    stage, recv, look, cache, cache_sem, send_sem, recv_sem, pass_sem, take_sem,
):
    z, y, c, x = place()
    dom = dom_of(z, y, c)
    right, left = lax.rem(x + 1, 4), lax.rem(x + 3, 4)

    def cache_copy(f):
        return pltpu.make_async_copy(
            cache_hbm.at[:, :, pl.ds(pl.multiple_of(f * WIDE, WIDE), WIDE)], cache.at[f], cache_sem.at[f]
        )

    for f in range(PHASES):
        cache_copy(f).start()

    barrier = pltpu.get_barrier_semaphore()

    @pl.loop(1, 32)
    def _(j):
        to = dom_of(lax.rem(z + j // 8, 4), lax.rem(y + lax.rem(j // 2, 4), 4), lax.rem(c + lax.rem(j, 2), 2))
        pl.semaphore_signal(barrier, inc=1, device_id=(to, x), device_id_type=MESH)

    for to in (right, left):
        pl.semaphore_signal(barrier, inc=1, device_id=(dom, to), device_id_type=MESH)
    pl.semaphore_wait(barrier, 33)

    def offset(i):
        group = lax.rem(x + i // 8, 4)
        t = lax.rem(i, 8)
        dz, dc = t // 2, lax.rem(t, 2)
        dy = lax.rem(group + 4 - dz, 4)
        return group * 8 + t, dz, dy, dc

    def dest(i):
        slot, dz, dy, dc = offset(i)
        return slot, dom_of(lax.rem(z + dz, 4), lax.rem(y + dy, 4), lax.rem(c + dc, 2))

    def fill(f):
        @pl.loop(0, SLOTS)
        def _(i):
            slot, to = dest(i)
            chosen = send_ref[0, to]
            gain = scale_ref[chosen] * MOMENTUM
            cols = pl.ds(pl.multiple_of(f * WIDE, WIDE), WIDE)
            stage[f, i] = (own_ref[chosen, :, cols].astype(F32) * gain).astype(BF16)

    def direct(f, i):
        slot, to = dest(i)
        return slot, pltpu.make_async_remote_copy(
            src_ref=stage.at[f, i], dst_ref=recv.at[f, slot],
            send_sem=send_sem.at[f, i], recv_sem=recv_sem.at[f, i],
            device_id=(to, x), device_id_type=MESH,
        )

    def local(f, i):
        return pltpu.make_async_copy(stage.at[f, i], recv.at[f, 0], recv_sem.at[f, i])

    def start(f, i):
        slot, copy = direct(f, i)

        @pl.when(slot == 0)
        def _():
            local(f, i).start()

        @pl.when(slot != 0)
        def _():
            copy.start()

    def arrive(f, i):
        slot, copy = direct(f, i)

        @pl.when(slot == 0)
        def _():
            local(f, i).wait()

        @pl.when(slot != 0)
        def _():
            copy.wait_recv()

    def onward(f, i):
        slot, _, _, _ = offset(i)
        to = jnp.where(i < 8, right, left)
        return pltpu.make_async_remote_copy(
            src_ref=recv.at[f, slot], dst_ref=recv.at[f, slot],
            send_sem=pass_sem.at[f, i], recv_sem=take_sem.at[f, i],
            device_id=(dom, to), device_id_type=MESH,
        )

    def taken(f, i):
        t = lax.rem(i, 8)
        slot = jnp.where(i < 8, lax.rem(x + 3, 4), lax.rem(x + 2, 4)) * 8 + t
        return pltpu.make_async_remote_copy(
            src_ref=recv.at[f, slot], dst_ref=recv.at[f, slot],
            send_sem=pass_sem.at[f, i], recv_sem=take_sem.at[f, i],
            device_id=(dom, right), device_id_type=MESH,
        )

    def finish(f):
        @pl.loop(0, SLOTS)
        def _(i):
            taken(f, i).wait_recv()

        cache_copy(f).wait()
        cols = pl.ds(pl.multiple_of(f * WIDE, WIDE), WIDE)

        @pl.loop(0, 8)
        def _(b):
            look[b] = (own_ref[b, :, cols].astype(F32) * scale_ref[b]).astype(BF16)

        @pl.loop(0, 32)
        def _(s):
            group, t = s // 8, lax.rem(s, 8)
            dz, dc = t // 2, lax.rem(t, 2)
            dy = lax.rem(group + 4 - dz, 4)
            src = dom_of(lax.rem(z + 4 - dz, 4), lax.rem(y + 4 - dy, 4), lax.rem(c + 2 - dc, 2))
            look[8 + src] = (
                recv[f, s].astype(F32) + (1.0 - MOMENTUM) * cache[f, src].astype(F32)
            ).astype(BF16)

        @pl.loop(0, 16)
        def _(t):
            coefs = jnp.concatenate([edge_ref[t, k] for k in range(6)], axis=1)
            rows = jnp.concatenate([look[near_ref[t, k]] for k in range(6)], axis=0)
            summed_ref[t, :, cols] = jnp.dot(coefs, rows, preferred_element_type=F32).astype(BF16)

    fill(0)

    @pl.loop(0, SLOTS)
    def _(i):
        start(0, i)

    @pl.loop(0, PHASES)
    def _(f):
        @pl.when(f + 1 < PHASES)
        def _():
            fill(f + 1)

        @pl.loop(0, SLOTS)
        def _(i):
            arrive(f, i)
            onward(f, i).start()

            @pl.when(f + 1 < PHASES)
            def _():
                start(f + 1, i)

        @pl.when(f >= 1)
        def _():
            finish(f - 1)

    finish(PHASES - 1)

    @pl.loop(0, PHASES)
    def _(f):
        @pl.loop(0, SLOTS)
        def _(i):
            slot, copy = direct(f, i)

            @pl.when(slot != 0)
            def _():
                copy.wait_send()

            onward(f, i).wait_send()


def exchange(own, scale, cache, send_list, near, edges):
    vmem = pl.BlockSpec(memory_space=pltpu.VMEM)
    smem = pl.BlockSpec(memory_space=pltpu.SMEM)
    return pl.pallas_call(
        halo_kernel,
        out_shape=jax.ShapeDtypeStruct((16, BLOCK, FEATS), BF16),
        in_specs=[smem, smem, smem, vmem, vmem, pl.BlockSpec(memory_space=pl.ANY)],
        out_specs=vmem,
        scratch_shapes=[
            pltpu.VMEM((PHASES, SLOTS, BLOCK, WIDE), BF16),
            pltpu.VMEM((PHASES, 32, BLOCK, WIDE), BF16),
            pltpu.VMEM((40, BLOCK, WIDE), BF16),
            pltpu.VMEM((PHASES, 32, BLOCK, WIDE), BF16),
            pltpu.SemaphoreType.DMA((PHASES,)),
            pltpu.SemaphoreType.DMA((PHASES, SLOTS)),
            pltpu.SemaphoreType.DMA((PHASES, SLOTS)),
            pltpu.SemaphoreType.DMA((PHASES, SLOTS)),
            pltpu.SemaphoreType.DMA((PHASES, SLOTS)),
        ],
        compiler_params=pltpu.CompilerParams(
            collective_id=0, has_side_effects=True, vmem_limit_bytes=56 * 2**20
        ),
        name="halo",
    )(send_list, scale.astype(F32), near, own.reshape(8, BLOCK, FEATS), edges, cache.reshape(32, BLOCK, FEATS))


ORDERS = ((2, 1, 0), (1, 0, 2), (0, 2, 1))


def scatter_kernel(factor, g_ref, out_ref, sent, got0, sum0, got1, sum1, got2, sum2, got3, send_sem, recv_sem):
    z, y, c, x = place()
    at = (z, y, x)

    def mate(axis, off):
        spot = [z, y, x]
        spot[axis] = lax.rem(spot[axis] + off, 4)
        return (dom_of(spot[0], spot[1], c), spot[2])

    other = (dom_of(z, y, 1 - c), x)
    barrier = pltpu.get_barrier_semaphore()
    pl.semaphore_signal(barrier, inc=1, device_id=other, device_id_type=MESH)
    for axis in range(3):
        for off in (1, 2, 3):
            pl.semaphore_signal(barrier, inc=1, device_id=mate(axis, off), device_id_type=MESH)
    pl.semaphore_wait(barrier, 10)

    def copy(src, dst, i, n, to):
        return pltpu.make_async_remote_copy(
            src_ref=src, dst_ref=dst, send_sem=send_sem.at[i, n], recv_sem=recv_sem.at[i, n],
            device_id=to, device_id_type=MESH,
        )

    def pick(ref, i, dims, axis, index):
        return ref.at[(i,) + tuple(index if d == axis else slice(None) for d in dims)]

    def load(ref, i, dims, axis, index):
        return ref[(i,) + tuple(index if d == axis else slice(None) for d in dims)]

    def cross(i):
        return copy(sent.at[i, 1 - c], got0.at[i], i, 0, other)

    def hop(i, stage, off):
        order = ORDERS[i % 3]
        axis = order[stage]
        dims = [d for d in (0, 1, 2) if d not in order[:stage]]
        src = (sum0, sum1, sum2)[stage]
        dst = (got1, got2, got3)[stage]
        goal = lax.rem(at[axis] + off, 4)
        return copy(pick(src, i, dims, axis, goal), dst.at[i, off - 1], i, 1 + 3 * stage + off - 1, mate(axis, off))

    def total(i, stage):
        order = ORDERS[i % 3]
        axis = order[stage]
        dims = [d for d in (0, 1, 2) if d not in order[:stage]]
        src = (sum0, sum1, sum2)[stage]
        dst = (got1, got2, got3)[stage]
        part = load(src, i, dims, axis, at[axis]).astype(F32)
        for off in range(3):
            part = part + dst[i, off].astype(F32)
        return part

    def make(i):
        part = g_ref[:, i * LANES:(i + 1) * LANES].astype(BF16).reshape(4, 4, 2, 4, 16, LANES)
        sent[i, 0] = part[:, :, 0]
        sent[i, 1] = part[:, :, 1]

    def step(i, stage):
        if stage == 0:
            make(i)
            cross(i).start()
        elif stage == 1:
            cross(i).wait_recv()
            sum0[i] = (sent[i, c].astype(F32) + got0[i].astype(F32)).astype(BF16)
            for off in (1, 2, 3):
                hop(i, 0, off).start()
        elif stage < 4:
            for off in (1, 2, 3):
                hop(i, stage - 2, off).wait_recv()
            (sum1, sum2)[stage - 2][i] = total(i, stage - 2).astype(BF16)
            for off in (1, 2, 3):
                hop(i, stage - 1, off).start()
        else:
            for off in (1, 2, 3):
                hop(i, 2, off).wait_recv()
            out_ref[:, i * LANES:(i + 1) * LANES] = total(i, 2) * factor

    for tick in range(SUBS + 4):
        for stage in (4, 3, 2, 1, 0):
            i = tick - stage
            if 0 <= i < SUBS:
                step(i, stage)

    for i in range(SUBS):
        cross(i).wait_send()
        for stage in range(3):
            for off in (1, 2, 3):
                hop(i, stage, off).wait_send()


def scatter(grads, factor):
    vmem = pl.BlockSpec(memory_space=pltpu.VMEM)
    return pl.pallas_call(
        functools.partial(scatter_kernel, factor),
        out_shape=jax.ShapeDtypeStruct((16, FEATS), F32),
        in_specs=[vmem],
        out_specs=vmem,
        scratch_shapes=[
            pltpu.VMEM((SUBS, 2, 4, 4, 4, 16, LANES), BF16),
            pltpu.VMEM((SUBS, 4, 4, 4, 16, LANES), BF16),
            pltpu.VMEM((SUBS, 4, 4, 4, 16, LANES), BF16),
            pltpu.VMEM((SUBS, 3, 4, 4, 16, LANES), BF16),
            pltpu.VMEM((SUBS, 4, 4, 16, LANES), BF16),
            pltpu.VMEM((SUBS, 3, 4, 16, LANES), BF16),
            pltpu.VMEM((SUBS, 4, 16, LANES), BF16),
            pltpu.VMEM((SUBS, 3, 16, LANES), BF16),
            pltpu.SemaphoreType.DMA((SUBS, 10)),
            pltpu.SemaphoreType.DMA((SUBS, 10)),
        ],
        compiler_params=pltpu.CompilerParams(
            collective_id=1, has_side_effects=True, vmem_limit_bytes=56 * 2**20
        ),
        name="scatter",
    )(grads)


def on_device(
    own_values, own_scale, halo_cache, send_list, batch_ids, neighbor_blocks, edge_tiles, w_self, w_neigh, cotangent,
):
    summed = exchange(own_values, own_scale, halo_cache, send_list, neighbor_blocks[0], edge_tiles[0])
    own_blocks = own_values.reshape(8, BLOCK, FEATS)
    own_deq = (own_blocks.astype(F32) * own_scale.astype(F32)[:, None, None]).astype(BF16)
    self_flat = jnp.take(own_deq, batch_ids[0], axis=0).reshape(-1, FEATS)
    summed_flat = summed.reshape(-1, FEATS)
    pre_act = jnp.dot(self_flat, w_self, preferred_element_type=F32) + jnp.dot(
        summed_flat, w_neigh, preferred_element_type=F32
    )
    sigmoid_z = jax.nn.sigmoid(pre_act)
    output_rows = (pre_act * sigmoid_z).astype(BF16)
    delta = (cotangent.astype(F32) * sigmoid_z * (1.0 + pre_act * (1.0 - sigmoid_z))).astype(BF16)
    stacked = jnp.concatenate([self_flat, summed_flat], axis=1)
    grads = lax.dot_general(stacked, delta, (((0,), (0,)), ((), ())), preferred_element_type=F32)
    rows = stacked.shape[0] * lax.axis_size("dom") * lax.axis_size("rep")
    return output_rows, scatter(grads, 1.0 / math.sqrt(rows))


def solution(mesh):
    placed = (
        P("dom", None), P("dom"), P("dom", None), P("dom", None), P("dom", "rep"), P("dom", "rep", None),
        P("dom", "rep", None, None, None), P(), P(), P(("dom", "rep"), None),
    )
    return jax.shard_map(
        on_device,
        mesh=mesh,
        in_specs=placed,
        out_specs=(P(("dom", "rep"), None), P(("dom", "rep"), None)),
        check_vma=False,
    )
```

```python
import functools
import math

import jax
import jax.numpy as jnp
from jax import lax
from jax.experimental import pallas as pl
from jax.experimental.pallas import tpu as pltpu
from jax.sharding import PartitionSpec as P

MOMENTUM = 0.6
MESH = pl.DeviceIdType.MESH
BLOCK = 128
FEATS = 1024
PHASES = 4
WIDE = FEATS // PHASES
PAIRS = 8
LANES = 128
TARGETS = 16
PIECE = (2, 4, 16, WIDE)
F32 = jnp.float32
BF16 = jnp.bfloat16
ORDERS = ((2, 1, 0), (1, 0, 2), (0, 2, 1))


def dom_of(z, y, c):
    return (z * 4 + y) * 2 + c


def columns(f):
    return pl.ds(pl.multiple_of(f * WIDE, WIDE), WIDE)


def layer_kernel(
    factor,
    send_ref, scale_ref, near_ref, self_ref, own_hbm, edge_hbm, cache_hbm, wself_hbm, wneigh_hbm, cot_hbm,
    out_hbm, grad_ref,
    own, edge, wself, wneigh, cache, cot, outs, deq, deq_t, base, look, acc, summed_t, delta,
    pool, recv, xfer, got0, got1, sum1, got2, sum2, got3,
    load_sem, cache_sem, cot_sem, out_sem,
    send_sem, recv_sem, swap_out, swap_in, pass_sem, take_sem, cross_out, cross_in, hop_out, hop_in,
):
    dom, x = lax.axis_index("dom"), lax.axis_index("rep")
    z, y, c = dom // 8, lax.rem(dom // 2, 4), lax.rem(dom, 2)
    right, left = lax.rem(x + 1, 4), lax.rem(x + 3, 4)
    other = (dom_of(z, y, 1 - c), x)

    loads = [
        pltpu.make_async_copy(src, dst, load_sem.at[n])
        for n, (src, dst) in enumerate(((own_hbm, own), (wself_hbm, wself), (wneigh_hbm, wneigh), (edge_hbm, edge)))
    ]

    def cache_copy(f):
        s = lax.rem(f, 2)
        return pltpu.make_async_copy(cache_hbm.at[:, :, columns(f)], cache.at[s], cache_sem.at[s])

    def cot_copy(n):
        return pltpu.make_async_copy(cot_hbm.at[:, :, columns(n)], cot.at[n % 2], cot_sem.at[n % 2])

    def out_copy(n):
        return pltpu.make_async_copy(outs.at[n % 2], out_hbm.at[:, :, columns(n)], out_sem.at[n % 2])

    for load in loads:
        load.start()
    for n in range(2):
        cache_copy(n).start()
        cot_copy(n).start()

    barrier = pltpu.get_barrier_semaphore()

    @pl.loop(1, 16)
    def _(j):
        to = dom_of(lax.rem(z + j // 4, 4), lax.rem(y + lax.rem(j, 4), 4), c)
        pl.semaphore_signal(barrier, inc=1, device_id=(to, x), device_id_type=MESH)

    @pl.loop(1, 4)
    def _(j):
        pl.semaphore_signal(barrier, inc=1, device_id=(dom, lax.rem(x + j, 4)), device_id_type=MESH)

    pl.semaphore_signal(barrier, inc=1, device_id=other, device_id_type=MESH)

    def offset(i):
        group, dz = lax.rem(x + lax.rem(i, 2), 4), i // 2
        return group, dz, lax.rem(group + 4 - dz, 4)

    def slot_of(group, dz, dc):
        return group * 8 + dz * 2 + dc

    def staged(f, i, w):
        return pool.at[f, i // 4, lax.rem(i, 4), pl.ds(2 * w, 2)]

    def handed(f, i):
        return xfer.at[f, i // 2, pl.ds(2 * lax.rem(i, 2), 2)]

    def fill(f):
        @pl.loop(0, PAIRS)
        def _(i):
            _, dz, dy = offset(i)
            for w in range(2):
                core = c if w == 0 else 1 - c
                chosen = send_ref[0, dom_of(lax.rem(z + dz, 4), lax.rem(y + dy, 4), core)]
                gain = scale_ref[chosen] * MOMENTUM
                rows = (own[chosen, :, columns(f)].astype(F32) * gain).astype(BF16)
                pool[f, i // 4, lax.rem(i, 4), pl.ds(2 * w, 2)] = rows.reshape(PIECE)

    def target(f, i, w):
        group, dz, _ = offset(i)
        return recv.at[f, slot_of(group, dz, 0)] if w == 0 else handed(f, i)

    def direct(f, i, w):
        _, dz, dy = offset(i)
        return pltpu.make_async_remote_copy(
            src_ref=staged(f, i, w), dst_ref=target(f, i, w),
            send_sem=send_sem.at[f, i, w], recv_sem=recv_sem.at[f, i, w],
            device_id=(dom_of(lax.rem(z + dz, 4), lax.rem(y + dy, 4), c), x), device_id_type=MESH,
        )

    def local(f, i, w):
        return pltpu.make_async_copy(staged(f, i, w), target(f, i, w), recv_sem.at[f, i, w])

    def stays(i):
        group, dz, _ = offset(i)
        return group * 4 + dz == 0

    def start(f, i):
        @pl.when(stays(i))
        def _():
            for w in range(2):
                local(f, i, w).start()

        @pl.when(jnp.logical_not(stays(i)))
        def _():
            for w in range(2):
                direct(f, i, w).start()

    def arrive(f, i, w):
        @pl.when(stays(i))
        def _():
            local(f, i, w).wait()

        @pl.when(jnp.logical_not(stays(i)))
        def _():
            direct(f, i, w).wait_recv()

    def swap(f, i):
        group, dz, _ = offset(i)
        return pltpu.make_async_remote_copy(
            src_ref=handed(f, i), dst_ref=recv.at[f, slot_of(group, dz, 1)],
            send_sem=swap_out.at[f, i], recv_sem=swap_in.at[f, i],
            device_id=other, device_id_type=MESH,
        )

    def onward(f, i, dc):
        group, dz, _ = offset(i)
        slot = slot_of(group, dz, dc)
        return pltpu.make_async_remote_copy(
            src_ref=recv.at[f, slot], dst_ref=recv.at[f, slot],
            send_sem=pass_sem.at[f, i, dc], recv_sem=take_sem.at[f, i, dc],
            device_id=(dom, jnp.where(lax.rem(i, 2) == 0, right, left)), device_id_type=MESH,
        )

    def taken(f, i, dc):
        group = lax.rem(x + 3 - lax.rem(i, 2), 4)
        slot = slot_of(group, i // 2, dc)
        return pltpu.make_async_remote_copy(
            src_ref=recv.at[f, slot], dst_ref=recv.at[f, slot],
            send_sem=pass_sem.at[f, i, dc], recv_sem=take_sem.at[f, i, dc],
            device_id=(dom, right), device_id_type=MESH,
        )

    def after_swap(f, i):
        swap(f, i).wait_recv()
        onward(f, i, 1).start()

    def prepare():
        @pl.loop(0, 8)
        def _(b):
            rows = (own[b].astype(F32) * scale_ref[b]).astype(BF16)
            deq[b] = rows
            deq_t[b] = rows.T

        loads[1].wait()

        @pl.loop(0, PHASES)
        def _(n):
            base[...] = jnp.dot(
                deq[...].reshape(FEATS, FEATS), wself[:, columns(n)], preferred_element_type=F32
            ).reshape(8, BLOCK, WIDE)

            @pl.loop(0, TARGETS)
            def _(t):
                acc[t, :, columns(n)] = base[self_ref[0, t]]

        loads[2].wait()
        loads[3].wait()

    def finish(f):
        @pl.loop(0, PAIRS)
        def _(i):
            for dc in range(2):
                taken(f, i, dc).wait_recv()

        cache_copy(f).wait()

        @pl.loop(0, 8)
        def _(b):
            look[b] = deq[b, :, columns(f)]

        @pl.loop(0, 32)
        def _(s):
            group, dz, dc = s // 8, lax.rem(s, 8) // 2, lax.rem(s, 2)
            dy = lax.rem(group + 4 - dz, 4)
            src = dom_of(lax.rem(z + 4 - dz, 4), lax.rem(y + 4 - dy, 4), lax.rem(c + dc, 2))
            fresh = recv[f, s].reshape(BLOCK, WIDE).astype(F32)
            look[8 + src] = (fresh + (1.0 - MOMENTUM) * cache[lax.rem(f, 2), src].astype(F32)).astype(BF16)

        @pl.when(f + 2 < PHASES)
        def _():
            cache_copy(f + 2).start()

        @pl.loop(0, 4)
        def _(g):
            parts = []
            for q in range(4):
                t = 4 * g + q
                coefs = jnp.concatenate([edge[t, k] for k in range(6)], axis=1)
                rows = jnp.concatenate([look[near_ref[t, k]] for k in range(6)], axis=0)
                part = jnp.dot(coefs, rows, preferred_element_type=F32).astype(BF16)
                summed_t[t, columns(f), :] = part.T
                parts.append(part)
            whole = jnp.concatenate(parts, axis=0)
            for n in range(PHASES):
                cols = slice(n * WIDE, (n + 1) * WIDE)
                more = jnp.dot(whole, wneigh[columns(f), cols], preferred_element_type=F32)
                acc[pl.ds(4 * g, 4), :, cols] += more.reshape(4, BLOCK, WIDE)

    loads[0].wait()
    fill(0)
    pl.semaphore_wait(barrier, 19)

    @pl.loop(0, PAIRS)
    def _(i):
        start(0, i)

    @pl.loop(0, PHASES)
    def _(f):
        @pl.when(f + 1 < PHASES)
        def _():
            fill(f + 1)

        @pl.loop(0, PAIRS)
        def _(i):
            arrive(f, i, 0)
            onward(f, i, 0).start()
            arrive(f, i, 1)
            swap(f, i).start()

            @pl.when(f + 1 < PHASES)
            def _():
                start(f + 1, i)

            @pl.when(i >= 1)
            def _():
                after_swap(f, i - 1)

        after_swap(f, PAIRS - 1)

        @pl.when(f == 0)
        def _():
            prepare()

        @pl.when(f >= 1)
        def _():
            finish(f - 1)

    finish(PHASES - 1)

    @pl.loop(0, PHASES)
    def _(f):
        @pl.loop(0, PAIRS)
        def _(i):
            @pl.when(jnp.logical_not(stays(i)))
            def _():
                for w in range(2):
                    direct(f, i, w).wait_send()

            swap(f, i).wait_send()

    at = (z, y, x)

    def mate(axis, off):
        spot = [z, y, x]
        spot[axis] = lax.rem(spot[axis] + off, 4)
        return (dom_of(spot[0], spot[1], c), spot[2])

    def cross(n, zz):
        return pltpu.make_async_remote_copy(
            src_ref=pool.at[n, 1 - c, zz], dst_ref=got0.at[n, zz],
            send_sem=cross_out.at[n, zz], recv_sem=cross_in.at[n, zz],
            device_id=other, device_id_type=MESH,
        )

    def plan(i, stage):
        order = ORDERS[i % 3]
        axis = order[stage]
        dims = [d for d in (0, 1, 2) if d not in order[:stage]]
        return axis, dims

    def hop(i, stage, off):
        axis, dims = plan(i, stage)
        goal = lax.rem(at[axis] + off, 4)
        cut = tuple(goal if d == axis else slice(None) for d in dims)
        if stage == 0:
            src = xfer.at[(i // 2,) + cut + (slice(None), pl.ds(i % 2 * LANES, LANES))]
        else:
            src = (sum1, sum2)[stage - 1].at[(i,) + cut]
        return pltpu.make_async_remote_copy(
            src_ref=src, dst_ref=(got1, got2, got3)[stage].at[i, off - 1],
            send_sem=hop_out.at[i, stage, off - 1], recv_sem=hop_in.at[i, stage, off - 1],
            device_id=mate(axis, off), device_id_type=MESH,
        )

    def total(i, stage):
        axis, dims = plan(i, stage)
        cut = tuple(at[axis] if d == axis else slice(None) for d in dims)
        if stage == 0:
            part = xfer[(i // 2,) + cut + (slice(None), slice(i % 2 * LANES, (i % 2 + 1) * LANES))]
        else:
            part = (sum1, sum2)[stage - 1][(i,) + cut]
        part = part.astype(F32)
        for off in range(3):
            part = part + (got1, got2, got3)[stage][i, off].astype(F32)
        return part

    def step(n, stage):
        if stage == 0:
            for zz in range(4):
                cross(n, zz).wait_recv()
                xfer[n, zz] = (pool[n, c, zz].astype(F32) + got0[n, zz].astype(F32)).astype(BF16)
        for i in (2 * n, 2 * n + 1):
            if stage > 0:
                for off in (1, 2, 3):
                    hop(i, stage - 1, off).wait_recv()
                part = total(i, stage - 1)
                if stage < 3:
                    (sum1, sum2)[stage - 1][i] = part.astype(BF16)
                else:
                    grad_ref[:, i * LANES:(i + 1) * LANES] = part * factor
            if stage < 3:
                for off in (1, 2, 3):
                    hop(i, stage, off).start()

    def activate(n, t):
        pre = acc[t, :, n * WIDE:(n + 1) * WIDE]
        gate = jax.nn.sigmoid(pre)
        outs[n % 2, t] = (pre * gate).astype(BF16)
        delta[n % 2, t] = (cot[n % 2, t].astype(F32) * gate * (1.0 + pre * (1.0 - gate))).astype(BF16)

    def before(n):
        cot_copy(n).wait()
        if n >= 2:
            out_copy(n - 2).wait()

    def after(n):
        out_copy(n).start()
        if n + 2 < PHASES:
            cot_copy(n + 2).start()

    before(0)

    @pl.loop(0, TARGETS)
    def _(t):
        activate(0, t)

    after(0)

    for n in range(PHASES):
        if n + 1 < PHASES:
            before(n + 1)
        for half in range(2):
            @pl.loop(0, 2)
            def _(m):
                rows = pl.ds(pl.multiple_of(m * 512, 512), 512)
                if half == 0:
                    lhs = [deq_t[self_ref[0, t], rows, :] for t in range(TARGETS)]
                else:
                    lhs = [summed_t[t, rows, :] for t in range(TARGETS)]
                part = jnp.dot(
                    jnp.concatenate(lhs, axis=1), delta[n % 2].reshape(TARGETS * BLOCK, WIDE),
                    preferred_element_type=F32,
                ).astype(BF16).reshape(4, 2, 4, 16, WIDE)
                zz = 2 * half + m
                for core in range(2):
                    pool[n, core, zz] = part[:, core]
                cross(n, zz).start()
                if n + 1 < PHASES:
                    for q in range(4):
                        activate(n + 1, 4 * zz + q)

            if half == 0:
                for stage in (3, 2, 1, 0):
                    if 0 <= n - 1 - stage:
                        step(n - 1 - stage, stage)
        if n + 1 < PHASES:
            after(n + 1)

    for tick in range(PHASES, PHASES + 4):
        for stage in (3, 2, 1, 0):
            if 0 <= tick - 1 - stage < PHASES:
                step(tick - 1 - stage, stage)

    out_copy(PHASES - 2).wait()
    out_copy(PHASES - 1).wait()

    @pl.loop(0, PHASES)
    def _(f):
        @pl.loop(0, PAIRS)
        def _(i):
            for dc in range(2):
                onward(f, i, dc).wait_send()

        @pl.loop(0, 4)
        def _(zz):
            cross(f, zz).wait_send()

    for i in range(2 * PHASES):
        for stage in range(3):
            for off in (1, 2, 3):
                hop(i, stage, off).wait_send()


def layer(factor, send_list, scale, near, batch, own, edges, cache, w_self, w_neigh, cot):
    vmem = pl.BlockSpec(memory_space=pltpu.VMEM)
    smem = pl.BlockSpec(memory_space=pltpu.SMEM)
    hbm = pl.BlockSpec(memory_space=pl.ANY)
    subs = 2 * PHASES
    dma = pltpu.SemaphoreType.DMA
    return pl.pallas_call(
        functools.partial(layer_kernel, factor),
        out_shape=(
            jax.ShapeDtypeStruct((TARGETS, BLOCK, FEATS), BF16),
            jax.ShapeDtypeStruct((16, FEATS), F32),
        ),
        in_specs=[smem] * 4 + [hbm] * 6,
        out_specs=(hbm, vmem),
        scratch_shapes=[
            pltpu.VMEM((8, BLOCK, FEATS), BF16),
            pltpu.VMEM((TARGETS, 6, BLOCK, BLOCK), BF16),
            pltpu.VMEM((FEATS, FEATS), BF16),
            pltpu.VMEM((FEATS, FEATS), BF16),
            pltpu.VMEM((2, 32, BLOCK, WIDE), BF16),
            pltpu.VMEM((2, TARGETS, BLOCK, WIDE), BF16),
            pltpu.VMEM((2, TARGETS, BLOCK, WIDE), BF16),
            pltpu.VMEM((8, BLOCK, FEATS), BF16),
            pltpu.VMEM((8, FEATS, BLOCK), BF16),
            pltpu.VMEM((8, BLOCK, WIDE), F32),
            pltpu.VMEM((40, BLOCK, WIDE), BF16),
            pltpu.VMEM((TARGETS, BLOCK, FEATS), F32),
            pltpu.VMEM((TARGETS, FEATS, BLOCK), BF16),
            pltpu.VMEM((2, TARGETS, BLOCK, WIDE), BF16),
            pltpu.VMEM((PHASES, 2, 4, 4, 4, 16, WIDE), BF16),
            pltpu.VMEM((PHASES, 32) + PIECE, BF16),
            pltpu.VMEM((PHASES, 4, 4, 4, 16, WIDE), BF16),
            pltpu.VMEM((PHASES, 4, 4, 4, 16, WIDE), BF16),
            pltpu.VMEM((subs, 3, 4, 4, 16, LANES), BF16),
            pltpu.VMEM((subs, 4, 4, 16, LANES), BF16),
            pltpu.VMEM((subs, 3, 4, 16, LANES), BF16),
            pltpu.VMEM((subs, 4, 16, LANES), BF16),
            pltpu.VMEM((subs, 3, 16, LANES), BF16),
            dma((4,)), dma((2,)), dma((2,)), dma((2,)),
            dma((PHASES, PAIRS, 2)), dma((PHASES, PAIRS, 2)), dma((PHASES, PAIRS)), dma((PHASES, PAIRS)),
            dma((PHASES, PAIRS, 2)), dma((PHASES, PAIRS, 2)), dma((PHASES, 4)), dma((PHASES, 4)),
            dma((subs, 3, 3)), dma((subs, 3, 3)),
        ],
        compiler_params=pltpu.CompilerParams(
            collective_id=0, has_side_effects=True, vmem_limit_bytes=62 * 2**20
        ),
        name="layer",
    )(send_list, scale, near, batch, own, edges, cache, w_self, w_neigh, cot)


def on_device(
    own_values, own_scale, halo_cache, send_list, batch_ids, neighbor_blocks, edge_tiles, w_self, w_neigh, cotangent,
):
    rows = cotangent.shape[0] * lax.axis_size("dom") * lax.axis_size("rep")
    output_rows, grads = layer(
        1.0 / math.sqrt(rows), send_list, own_scale.astype(F32), neighbor_blocks[0], batch_ids,
        own_values.reshape(8, BLOCK, FEATS), edge_tiles[0], halo_cache.reshape(32, BLOCK, FEATS),
        w_self, w_neigh, cotangent.reshape(TARGETS, BLOCK, FEATS),
    )
    return output_rows.reshape(-1, FEATS), grads


def solution(mesh):
    placed = (
        P("dom", None), P("dom"), P("dom", None), P("dom", None), P("dom", "rep"), P("dom", "rep", None),
        P("dom", "rep", None, None, None), P(), P(), P(("dom", "rep"), None),
    )
    return jax.shard_map(
        on_device,
        mesh=mesh,
        in_specs=placed,
        out_specs=(P(("dom", "rep"), None), P(("dom", "rep"), None)),
        check_vma=False,
    )
```

```python
import functools
import math

import jax
import jax.numpy as jnp
from jax import lax
from jax.experimental import pallas as pl
from jax.experimental.pallas import tpu as pltpu
from jax.sharding import PartitionSpec as P

MOMENTUM = 0.6
MESH = pl.DeviceIdType.MESH
BLOCK = 128
FEATS = 1024
PHASES = 4
WIDE = FEATS // PHASES
PAIRS = 8
LANES = 128
TARGETS = 16
PIECE = (2, 4, 16, WIDE)
PAIR_LAG = 2
HOP_LAG = 4
F32 = jnp.float32
BF16 = jnp.bfloat16


def dom_of(z, y, c):
    return (z * 4 + y) * 2 + c


def columns(f):
    return pl.ds(pl.multiple_of(f * WIDE, WIDE), WIDE)


def layer_kernel(
    factor,
    send_ref, near_ref, self_ref, scale_vmem, own_hbm, edge_hbm, cache_hbm, wself_hbm, wneigh_hbm, cot_hbm,
    out_hbm, grad_ref,
    own, edge, wself, wneigh, cache, cot, outs, base, look, acc, both_t, delta,
    pool, recv, xfer, got0, got1, sum1, got2, scale_ref,
    load_sem, cache_sem, cot_sem, out_sem,
    send_sem, recv_sem, swap_out, swap_in, pass_sem, take_sem, cross_out, cross_in, hop_out, hop_in, last_out, last_in,
):
    dom, x = lax.axis_index("dom"), lax.axis_index("rep")
    z, y, c = dom // 8, lax.rem(dom // 2, 4), lax.rem(dom, 2)
    right, left = lax.rem(x + 1, 4), lax.rem(x + 3, 4)
    other = (dom_of(z, y, 1 - c), x)

    loads = [
        pltpu.make_async_copy(src, dst, load_sem.at[n])
        for n, (src, dst) in enumerate(((own_hbm, own), (wself_hbm, wself), (wneigh_hbm, wneigh), (edge_hbm, edge)))
    ]

    def cache_copy(f):
        s = lax.rem(f, 2)
        return pltpu.make_async_copy(cache_hbm.at[:, :, columns(f)], cache.at[s], cache_sem.at[s])

    def cot_copy(n):
        return pltpu.make_async_copy(cot_hbm.at[:, :, columns(n)], cot.at[n % 2], cot_sem.at[n % 2])

    def out_copy(n):
        return pltpu.make_async_copy(outs.at[n % 2], out_hbm.at[:, :, columns(n)], out_sem.at[n % 2])

    loads[0].start()

    barrier = pltpu.get_barrier_semaphore()

    @pl.loop(1, 16)
    def _(j):
        to = dom_of(lax.rem(z + j // 4, 4), lax.rem(y + lax.rem(j, 4), 4), c)
        pl.semaphore_signal(barrier, inc=1, device_id=(to, x), device_id_type=MESH)

    @pl.loop(0, 12)
    def _(j):
        to = (dom_of(lax.rem(z + j // 3, 4), y, c), lax.rem(x + 1 + lax.rem(j, 3), 4))
        pl.semaphore_signal(barrier, inc=1, device_id=to, device_id_type=MESH)

    pl.semaphore_signal(barrier, inc=1, device_id=other, device_id_type=MESH)

    def offset(i):
        group, dz = lax.rem(x + lax.rem(i, 2), 4), i // 2
        return group, dz, lax.rem(group + 4 - dz, 4)

    def slot_of(group, dz, dc):
        return group * 8 + dz * 2 + dc

    def staged(f, i, w):
        return pool.at[f, i // 4, lax.rem(i, 4), pl.ds(2 * w, 2)]

    def handed(f, i):
        return xfer.at[f, i // 2, pl.ds(2 * lax.rem(i, 2), 2)]

    def target(f, i, w):
        group, dz, _ = offset(i)
        return recv.at[f, slot_of(group, dz, 0)] if w == 0 else handed(f, i)

    def direct(f, i, w):
        _, dz, dy = offset(i)
        return pltpu.make_async_remote_copy(
            src_ref=staged(f, i, w), dst_ref=target(f, i, w),
            send_sem=send_sem.at[f, i, w], recv_sem=recv_sem.at[f, i, w],
            device_id=(dom_of(lax.rem(z + dz, 4), lax.rem(y + dy, 4), c), x), device_id_type=MESH,
        )

    def leaves(i):
        group, dz, _ = offset(i)
        return group * 4 + dz != 0

    def fill(f):
        @pl.loop(0, PAIRS)
        def _(i):
            _, dz, dy = offset(i)
            pieces = []
            for core in (c, 1 - c):
                chosen = send_ref[0, dom_of(lax.rem(z + dz, 4), lax.rem(y + dy, 4), core)]
                gain = scale_ref[chosen] * MOMENTUM
                pieces.append((own[chosen, :, columns(f)].astype(F32) * gain).astype(BF16).reshape(PIECE))

            @pl.when(leaves(i))
            def _():
                for w in range(2):
                    pool[f, i // 4, lax.rem(i, 4), pl.ds(2 * w, 2)] = pieces[w]

            @pl.when(jnp.logical_not(leaves(i)))
            def _():
                recv[f, 0] = pieces[0]
                xfer[f, i // 2, pl.ds(2 * lax.rem(i, 2), 2)] = pieces[1]

    def send(f, i, w):
        @pl.when(leaves(i))
        def _():
            direct(f, i, w).start()

    def arrive(f, i, w):
        @pl.when(leaves(i))
        def _():
            direct(f, i, w).wait_recv()

    def swap(f, i):
        group, dz, _ = offset(i)
        return pltpu.make_async_remote_copy(
            src_ref=handed(f, i), dst_ref=recv.at[f, slot_of(group, dz, 1)],
            send_sem=swap_out.at[f, i], recv_sem=swap_in.at[f, i],
            device_id=other, device_id_type=MESH,
        )

    def onward(f, i, dc):
        group, dz, _ = offset(i)
        slot = slot_of(group, dz, dc)
        return pltpu.make_async_remote_copy(
            src_ref=recv.at[f, slot], dst_ref=recv.at[f, slot],
            send_sem=pass_sem.at[f, i, dc], recv_sem=take_sem.at[f, i, dc],
            device_id=(dom, jnp.where(lax.rem(i, 2) == 0, right, left)), device_id_type=MESH,
        )

    def taken(f, i, dc):
        group = lax.rem(x + 3 - lax.rem(i, 2), 4)
        slot = slot_of(group, i // 2, dc)
        return pltpu.make_async_remote_copy(
            src_ref=recv.at[f, slot], dst_ref=recv.at[f, slot],
            send_sem=pass_sem.at[f, i, dc], recv_sem=take_sem.at[f, i, dc],
            device_id=(dom, right), device_id_type=MESH,
        )

    def after_swap(f, i):
        swap(f, i).wait_recv()
        onward(f, i, 1).start()
        group, dz, _ = offset(i)
        combine(f, group, dz, 1)

    def dequantize(b):
        rows = (own[b].astype(F32) * scale_ref[b]).astype(BF16)
        own[b] = rows
        both_t[b] = rows.T

    def begin(n):
        base[...] = jnp.dot(
            own[...].reshape(FEATS, FEATS), wself[:, columns(n)], preferred_element_type=F32
        ).reshape(8, BLOCK, WIDE)

        @pl.loop(0, TARGETS)
        def _(t):
            acc[t, :, columns(n)] = base[self_ref[0, t]]

    def combine(f, group, dz, dc):
        dy = lax.rem(group + 4 - dz, 4)
        src = dom_of(lax.rem(z + 4 - dz, 4), lax.rem(y + 4 - dy, 4), c if dc == 0 else 1 - c)
        fresh = recv[f, slot_of(group, dz, dc)].reshape(BLOCK, WIDE).astype(F32)
        side = lax.rem(f, 2)
        look[side, 8 + src] = (fresh + (1.0 - MOMENTUM) * cache[side, src].astype(F32)).astype(BF16)

    def combine_taken(f, i):
        for dc in (1, 0):
            taken(f, i, dc).wait_recv()
            combine(f, lax.rem(x + 3 - lax.rem(i, 2), 4), i // 2, dc)

    def aggregate(f, g):
        parts = []
        for q in range(4):
            t = 4 * g + q
            coefs = jnp.concatenate([edge[t, k] for k in range(6)], axis=1)
            rows = jnp.concatenate([look[lax.rem(f, 2), near_ref[k, 0, t]] for k in range(6)], axis=0)
            part = jnp.dot(coefs, rows, preferred_element_type=F32).astype(BF16)
            both_t[8 + t, columns(f), :] = part.T
            parts.append(part)
        whole = jnp.concatenate(parts, axis=0)
        for n in range(PHASES):
            cols = slice(n * WIDE, (n + 1) * WIDE)
            more = jnp.dot(whole, wneigh[columns(f), cols], preferred_element_type=F32)
            acc[pl.ds(4 * g, 4), :, cols] += more.reshape(4, BLOCK, WIDE)

    lane = lax.broadcasted_iota(jnp.int32, (1, 8), 1)
    for b in range(8):
        scale_ref[b] = jnp.sum(jnp.where(lane == b, scale_vmem[...].astype(F32), 0.0))

    loads[0].wait()
    fill(0)
    pl.semaphore_wait(barrier, 28)
    for f in range(PHASES):
        if f:
            fill(f)
        for w in (1, 0):
            @pl.loop(0, PAIRS)
            def _(i):
                send(f, i, w)

        if f == 0:
            for n in range(2):
                cache_copy(n).start()

    for load in loads[1:]:
        load.start()
    for n in range(2):
        cot_copy(n).start()

    @pl.loop(0, PHASES)
    def _(f):
        cache_copy(f).wait()

        @pl.loop(0, PAIRS)
        def _(i):
            arrive(f, i, 1)
            swap(f, i).start()

            @pl.when(i >= 1)
            def _():
                after_swap(f, i - 1)

            @pl.when(f == 0)
            def _():
                dequantize(i)

            @pl.when((f == 1) & (i == 0))
            def _():
                for load in loads[1:]:
                    load.wait()

            @pl.when((f == 1) & (i < PHASES))
            def _():
                begin(i)

            @pl.when(f >= 1)
            def _():
                combine_taken(f - 1, i)

        @pl.loop(0, PAIRS)
        def _(i):
            arrive(f, i, 0)
            onward(f, i, 0).start()

            @pl.when(i == 0)
            def _():
                after_swap(f, PAIRS - 1)

            group, dz, _ = offset(i)
            combine(f, group, dz, 0)
            look[lax.rem(f, 2), i] = own[i, :, columns(f)]

            @pl.when((f >= 1) & (i == 0) & (f + 1 < PHASES))
            def _():
                cache_copy(f + 1).start()

            @pl.when((f >= 1) & (lax.rem(i, 2) == 0))
            def _():
                aggregate(f - 1, i // 2)

    @pl.loop(0, PAIRS)
    def _(i):
        combine_taken(PHASES - 1, i)

    @pl.loop(0, 4)
    def _(g):
        aggregate(PHASES - 1, g)

    @pl.loop(0, PHASES)
    def _(f):
        @pl.loop(0, PAIRS)
        def _(i):
            @pl.when(leaves(i))
            def _():
                for w in range(2):
                    direct(f, i, w).wait_send()

            swap(f, i).wait_send()

    def cross(n, zz):
        return pltpu.make_async_remote_copy(
            src_ref=pool.at[n, 1 - c, zz], dst_ref=got0.at[n, zz],
            send_sem=cross_out.at[n, zz], recv_sem=cross_in.at[n, zz],
            device_id=other, device_id_type=MESH,
        )

    def hop(n, h, zz, off):
        lanes = pl.ds(h * LANES, LANES)
        if h == 0:
            goal = lax.rem(x + off, 4)
            src, to = xfer.at[n, zz, :, goal, :, lanes], (dom, goal)
        else:
            goal = lax.rem(y + off, 4)
            src, to = xfer.at[n, zz, goal, :, :, lanes], (dom_of(z, goal, c), x)
        return pltpu.make_async_remote_copy(
            src_ref=src, dst_ref=got1.at[n, h, off - 1, zz],
            send_sem=hop_out.at[n, h, zz, off - 1], recv_sem=hop_in.at[n, h, zz, off - 1],
            device_id=to, device_id_type=MESH,
        )

    def last(n, h, zz, k, j):
        goal = lax.rem((y if h == 0 else x) + k, 4)
        to = (dom_of(zz, goal, c), x) if h == 0 else (dom_of(zz, y, c), goal)
        return pltpu.make_async_remote_copy(
            src_ref=sum1.at[n, h, zz, goal], dst_ref=got2.at[n, h, j],
            send_sem=last_out.at[n, h, j], recv_sem=last_in.at[n, h, j],
            device_id=to, device_id_type=MESH,
        )

    def pair_up(tile):
        n, zz = tile // 4, lax.rem(tile, 4)
        cross(n, zz).wait_recv()
        xfer[n, zz] = (pool[n, c, zz].astype(F32) + got0[n, zz].astype(F32)).astype(BF16)
        for off in (2, 1, 3):
            for h in range(2):
                hop(n, h, zz, off).start()

    def spread(tile):
        n, zz = tile // 4, lax.rem(tile, 4)
        for h in range(2):
            for off in (1, 2, 3):
                hop(n, h, zz, off).wait_recv()
            mine = (xfer[n, zz, :, x] if h == 0 else xfer[n, zz, y])[:, :, h * LANES:(h + 1) * LANES].astype(F32)
            for off in range(3):
                mine = mine + got1[n, h, off, zz].astype(F32)
            sum1[n, h, zz] = mine.astype(BF16)
        dz = lax.rem(zz + 4 - z, 4)
        for k in (2, 1, 3):
            for h in range(2):
                last(n, h, zz, k, dz * 4 + k).start()

        @pl.when(dz != 0)
        def _():
            for h in range(2):
                last(n, h, zz, 0, dz * 4).start()

    def close(n):
        for h in range(2):
            @pl.loop(1, 16)
            def _(j):
                last(n, h, lax.rem(z + j // 4, 4), lax.rem(j, 4), j).wait_recv()

            part = sum1[n, h, z, y if h == 0 else x].astype(F32)
            for j in range(1, 16):
                part = part + got2[n, h, j].astype(F32)
            grad_ref[:, (2 * n + h) * LANES:(2 * n + h + 1) * LANES] = part * factor

    def activate(n, t):
        pre = acc[t, :, n * WIDE:(n + 1) * WIDE]
        gate = jax.nn.sigmoid(pre)
        outs[n % 2, t] = (pre * gate).astype(BF16)
        delta[n % 2, t] = (cot[n % 2, t].astype(F32) * gate * (1.0 + pre * (1.0 - gate))).astype(BF16)

    def before(n):
        cot_copy(n).wait()
        if n >= 2:
            out_copy(n - 2).wait()

    def after(n):
        out_copy(n).start()
        if n + 2 < PHASES:
            cot_copy(n + 2).start()

    before(0)

    @pl.loop(0, TARGETS)
    def _(t):
        activate(0, t)

    after(0)

    for n in range(PHASES):
        if n + 1 < PHASES:
            before(n + 1)

        @pl.loop(0, 4)
        def _(zz):
            rows = pl.ds(pl.multiple_of(lax.rem(zz, 2) * 512, 512), 512)
            lhs = [both_t[jnp.where(zz < 2, self_ref[0, t], 8 + t), rows, :] for t in range(TARGETS)]
            part = jnp.dot(
                jnp.concatenate(lhs, axis=1), delta[n % 2].reshape(TARGETS * BLOCK, WIDE),
                preferred_element_type=F32,
            ).astype(BF16).reshape(4, 2, 4, 16, WIDE)
            for core in range(2):
                pool[n, core, zz] = part[:, core]
            cross(n, zz).start()
            if n + 1 < PHASES:
                for q in range(4):
                    activate(n + 1, 4 * zz + q)

            tile = 4 * n + zz

            @pl.when(tile >= PAIR_LAG)
            def _():
                pair_up(tile - PAIR_LAG)

            @pl.when(tile >= PAIR_LAG + HOP_LAG)
            def _():
                spread(tile - PAIR_LAG - HOP_LAG)

        if n + 1 < PHASES:
            after(n + 1)

    tiles = 4 * PHASES
    for tile in range(tiles - PAIR_LAG, tiles):
        pair_up(jnp.int32(tile))

    @pl.loop(tiles - PAIR_LAG - HOP_LAG, tiles)
    def _(tile):
        spread(tile)

    for n in range(PHASES):
        close(n)

    out_copy(PHASES - 2).wait()
    out_copy(PHASES - 1).wait()

    @pl.loop(0, PHASES)
    def _(f):
        @pl.loop(0, PAIRS)
        def _(i):
            for dc in range(2):
                onward(f, i, dc).wait_send()

        @pl.loop(0, 4)
        def _(zz):
            cross(f, zz).wait_send()
            for h in range(2):
                for off in (1, 2, 3):
                    hop(f, h, zz, off).wait_send()

        for h in range(2):
            @pl.loop(1, 16)
            def _(j):
                last(f, h, lax.rem(z + j // 4, 4), lax.rem(j, 4), j).wait_send()


def layer(factor, send_list, near, batch, scale, own, edges, cache, w_self, w_neigh, cot):
    vmem = pl.BlockSpec(memory_space=pltpu.VMEM)
    smem = pl.BlockSpec(memory_space=pltpu.SMEM)
    hbm = pl.BlockSpec(memory_space=pl.ANY)
    dma = pltpu.SemaphoreType.DMA
    return pl.pallas_call(
        functools.partial(layer_kernel, factor),
        out_shape=(
            jax.ShapeDtypeStruct((TARGETS, BLOCK, FEATS), BF16),
            jax.ShapeDtypeStruct((16, FEATS), F32),
        ),
        in_specs=[smem] * 3 + [vmem] + [hbm] * 6,
        out_specs=(hbm, vmem),
        scratch_shapes=[
            pltpu.VMEM((8, BLOCK, FEATS), BF16),
            pltpu.VMEM((TARGETS, 6, BLOCK, BLOCK), BF16),
            pltpu.VMEM((FEATS, FEATS), BF16),
            pltpu.VMEM((FEATS, FEATS), BF16),
            pltpu.VMEM((2, 32, BLOCK, WIDE), BF16),
            pltpu.VMEM((2, TARGETS, BLOCK, WIDE), BF16),
            pltpu.VMEM((2, TARGETS, BLOCK, WIDE), BF16),
            pltpu.VMEM((8, BLOCK, WIDE), F32),
            pltpu.VMEM((2, 40, BLOCK, WIDE), BF16),
            pltpu.VMEM((TARGETS, BLOCK, FEATS), F32),
            pltpu.VMEM((8 + TARGETS, FEATS, BLOCK), BF16),
            pltpu.VMEM((2, TARGETS, BLOCK, WIDE), BF16),
            pltpu.VMEM((PHASES, 2, 4, 4, 4, 16, WIDE), BF16),
            pltpu.VMEM((PHASES, 32) + PIECE, BF16),
            pltpu.VMEM((PHASES, 4, 4, 4, 16, WIDE), BF16),
            pltpu.VMEM((PHASES, 4, 4, 4, 16, WIDE), BF16),
            pltpu.VMEM((PHASES, 2, 3, 4, 4, 16, LANES), BF16),
            pltpu.VMEM((PHASES, 2, 4, 4, 16, LANES), BF16),
            pltpu.VMEM((PHASES, 2, 16, 16, LANES), BF16),
            pltpu.SMEM((8,), F32),
            dma((4,)), dma((2,)), dma((2,)), dma((2,)),
            dma((PHASES, PAIRS, 2)), dma((PHASES, PAIRS, 2)), dma((PHASES, PAIRS)), dma((PHASES, PAIRS)),
            dma((PHASES, PAIRS, 2)), dma((PHASES, PAIRS, 2)), dma((PHASES, 4)), dma((PHASES, 4)),
            dma((PHASES, 2, 4, 3)), dma((PHASES, 2, 4, 3)), dma((PHASES, 2, 16)), dma((PHASES, 2, 16)),
        ],
        compiler_params=pltpu.CompilerParams(
            collective_id=0, has_side_effects=True, vmem_limit_bytes=62 * 2**20
        ),
        name="layer",
    )(send_list, near, batch, scale, own, edges, cache, w_self, w_neigh, cot)


def on_device(
    own_values, own_scale, halo_cache, send_list, batch_ids, neighbor_blocks, edge_tiles, w_self, w_neigh, cotangent,
):
    rows = cotangent.shape[0] * lax.axis_size("dom") * lax.axis_size("rep")
    output_rows, grads = layer(
        1.0 / math.sqrt(rows), send_list, neighbor_blocks.transpose(2, 0, 1), batch_ids, own_scale.reshape(1, 8),
        own_values.reshape(8, BLOCK, FEATS), edge_tiles[0], halo_cache.reshape(32, BLOCK, FEATS),
        w_self, w_neigh, cotangent.reshape(TARGETS, BLOCK, FEATS),
    )
    return output_rows.reshape(-1, FEATS), grads


def solution(mesh):
    placed = (
        P("dom", None), P("dom"), P("dom", None), P("dom", None), P("dom", "rep"), P("dom", "rep", None),
        P("dom", "rep", None, None, None), P(), P(), P(("dom", "rep"), None),
    )
    return jax.shard_map(
        on_device,
        mesh=mesh,
        in_specs=placed,
        out_specs=(P(("dom", "rep"), None), P(("dom", "rep"), None)),
        check_vma=False,
    )
```

```python
import functools
import math

import jax
import jax.numpy as jnp
from jax import lax
from jax.experimental import pallas as pl
from jax.experimental.pallas import tpu as pltpu
from jax.sharding import PartitionSpec as P

MOMENTUM = 0.6
MESH = pl.DeviceIdType.MESH
BLOCK = 128
FEATS = 1024
PHASES = 4
WIDE = FEATS // PHASES
PAIRS = 8
TARGETS = 16
PIECE = (2, 4, 16, WIDE)
SWAP_LAG = 2
F32 = jnp.float32
BF16 = jnp.bfloat16


def dom_of(z, y, c):
    return (z * 4 + y) * 2 + c


def columns(f):
    return pl.ds(pl.multiple_of(f * WIDE, WIDE), WIDE)


def layer_kernel(
    factor,
    send_ref, near_ref, self_ref, scale_vmem, own_hbm, edge_hbm, cache_hbm, wself_hbm, wneigh_hbm, cot_hbm,
    out_ref, grad_ref,
    own, edge, wneigh, cache, cot, base, look, acc, both_t, delta,
    pool, recv, xfer, got0, got1, sum1, got2, scale_ref,
    load_sem, wself_sem, cache_sem, cot_sem,
    send_sem, recv_sem, swap_out, swap_in, pass_sem, take_sem, cross_out, cross_in, hop_out, hop_in, last_out, last_in,
):
    dom, x = lax.axis_index("dom"), lax.axis_index("rep")
    z, y, c = dom // 8, lax.rem(dom // 2, 4), lax.rem(dom, 2)
    right, left = lax.rem(x + 1, 4), lax.rem(x + 3, 4)
    other = (dom_of(z, y, 1 - c), x)

    loads = [
        pltpu.make_async_copy(src, dst, load_sem.at[n])
        for n, (src, dst) in enumerate(((own_hbm, own), (wneigh_hbm, wneigh), (edge_hbm, edge)))
    ]

    def wself(n):
        return delta.at[n // 2, pl.ds(lax.rem(n, 2) * 8, 8)]

    def wself_copy(n):
        return pltpu.make_async_copy(wself_hbm.at[:, :, columns(n)], wself(n), wself_sem.at[n])

    def cache_copy(f):
        s = lax.rem(f, 2)
        return pltpu.make_async_copy(cache_hbm.at[:, :, columns(f)], cache.at[s], cache_sem.at[s])

    def cot_copy(n):
        return pltpu.make_async_copy(cot_hbm.at[:, :, columns(n)], cot.at[n % 2], cot_sem.at[n % 2])

    loads[0].start()

    barrier = pltpu.get_barrier_semaphore()

    @pl.loop(1, 16)
    def _(j):
        to = dom_of(lax.rem(z + j // 4, 4), lax.rem(y + lax.rem(j, 4), 4), c)
        pl.semaphore_signal(barrier, inc=1, device_id=(to, x), device_id_type=MESH)

    @pl.loop(0, 12)
    def _(j):
        to = (dom_of(lax.rem(z + j // 3, 4), y, c), lax.rem(x + 1 + lax.rem(j, 3), 4))
        pl.semaphore_signal(barrier, inc=1, device_id=to, device_id_type=MESH)

    pl.semaphore_signal(barrier, inc=1, device_id=other, device_id_type=MESH)

    def offset(i):
        group, dz = lax.rem(x + lax.rem(i, 2), 4), i // 2
        return group, dz, lax.rem(group + 4 - dz, 4)

    def slot_of(group, dz, dc):
        return group * 8 + dz * 2 + dc

    def staged(f, i, w):
        return pool.at[f, i // 4, lax.rem(i, 4), pl.ds(2 * w, 2)]

    def handed(f, i):
        return xfer.at[f, i // 2, pl.ds(2 * lax.rem(i, 2), 2)]

    def target(f, i, w):
        group, dz, _ = offset(i)
        return recv.at[f, slot_of(group, dz, 0)] if w == 0 else handed(f, i)

    def direct(f, i, w):
        _, dz, dy = offset(i)
        return pltpu.make_async_remote_copy(
            src_ref=staged(f, i, w), dst_ref=target(f, i, w),
            send_sem=send_sem.at[i], recv_sem=recv_sem.at[f, i, w],
            device_id=(dom_of(lax.rem(z + dz, 4), lax.rem(y + dy, 4), c), x), device_id_type=MESH,
        )

    def leaves(i):
        group, dz, _ = offset(i)
        return group * 4 + dz != 0

    def fill(f):
        @pl.loop(0, PAIRS)
        def _(i):
            _, dz, dy = offset(i)
            pieces = []
            for core in (c, 1 - c):
                chosen = send_ref[0, dom_of(lax.rem(z + dz, 4), lax.rem(y + dy, 4), core)]
                gain = scale_ref[chosen] * MOMENTUM
                pieces.append((own[chosen, :, columns(f)].astype(F32) * gain).astype(BF16).reshape(PIECE))

            @pl.when(leaves(i))
            def _():
                for w in range(2):
                    pool[f, i // 4, lax.rem(i, 4), pl.ds(2 * w, 2)] = pieces[w]

            @pl.when(jnp.logical_not(leaves(i)))
            def _():
                recv[f, 0] = pieces[0]
                xfer[f, i // 2, pl.ds(2 * lax.rem(i, 2), 2)] = pieces[1]

    def send(f, i, w):
        @pl.when(leaves(i))
        def _():
            direct(f, i, w).start()

    def arrive(f, i, w):
        @pl.when(leaves(i))
        def _():
            direct(f, i, w).wait_recv()

    def swap(f, i):
        group, dz, _ = offset(i)
        return pltpu.make_async_remote_copy(
            src_ref=handed(f, i), dst_ref=recv.at[f, slot_of(group, dz, 1)],
            send_sem=swap_out, recv_sem=swap_in.at[f, i],
            device_id=other, device_id_type=MESH,
        )

    def onward(f, i, dc):
        group, dz, _ = offset(i)
        slot = slot_of(group, dz, dc)
        return pltpu.make_async_remote_copy(
            src_ref=recv.at[f, slot], dst_ref=recv.at[f, slot],
            send_sem=pass_sem, recv_sem=take_sem.at[f, i],
            device_id=(dom, jnp.where(lax.rem(i, 2) == 0, right, left)), device_id_type=MESH,
        )

    def taken(f, i):
        both = recv.at[f, pl.ds(slot_of(lax.rem(x + 3 - lax.rem(i, 2), 4), i // 2, 0), 2)]
        return pltpu.make_async_copy(both, both, take_sem.at[f, i])

    def after_swap(f, i):
        swap(f, i).wait_recv()
        onward(f, i, 1).start()
        group, dz, _ = offset(i)
        combine(f, group, dz, 1)

    def dequantize(b):
        rows = (own[b].astype(F32) * scale_ref[b]).astype(BF16)
        own[b] = rows
        both_t[b] = rows.T

    def begin(n):
        wself_copy(n).wait()
        base[...] = jnp.dot(
            own[...].reshape(FEATS, FEATS), wself(n)[...].reshape(FEATS, WIDE), preferred_element_type=F32
        ).reshape(8, BLOCK, WIDE)

        @pl.loop(0, TARGETS)
        def _(t):
            acc[t, :, columns(n)] = base[self_ref[0, t]]

    def combine(f, group, dz, dc):
        dy = lax.rem(group + 4 - dz, 4)
        src = dom_of(lax.rem(z + 4 - dz, 4), lax.rem(y + 4 - dy, 4), c if dc == 0 else 1 - c)
        fresh = recv[f, slot_of(group, dz, dc)].reshape(BLOCK, WIDE).astype(F32)
        side = lax.rem(f, 2)
        look[side, 8 + src] = (fresh + (1.0 - MOMENTUM) * cache[side, src].astype(F32)).astype(BF16)

    def combine_taken(f, i):
        taken(f, i).wait()
        for dc in range(2):
            combine(f, lax.rem(x + 3 - lax.rem(i, 2), 4), i // 2, dc)

    def aggregate(f, g):
        parts = []
        for q in range(4):
            t = 4 * g + q
            coefs = jnp.concatenate([edge[t, k] for k in range(6)], axis=1)
            rows = jnp.concatenate([look[lax.rem(f, 2), near_ref[k, 0, t]] for k in range(6)], axis=0)
            part = jnp.dot(coefs, rows, preferred_element_type=F32).astype(BF16)
            both_t[8 + t, columns(f), :] = part.T
            parts.append(part)
        whole = jnp.concatenate(parts, axis=0)
        for n in range(PHASES):
            cols = slice(n * WIDE, (n + 1) * WIDE)
            more = jnp.dot(whole, wneigh[columns(f), cols], preferred_element_type=F32)
            acc[pl.ds(4 * g, 4), :, cols] += more.reshape(4, BLOCK, WIDE)

    lane = lax.broadcasted_iota(jnp.int32, (1, 8), 1)
    for b in range(8):
        scale_ref[b] = jnp.sum(jnp.where(lane == b, scale_vmem[...].astype(F32), 0.0))

    loads[0].wait()
    fill(0)
    pl.semaphore_wait(barrier, 28)
    for f in range(PHASES):
        if f:
            fill(f)
        for w in (1, 0):
            @pl.loop(0, PAIRS)
            def _(i):
                send(f, i, w)

        if f == 0:
            for n in range(2):
                cache_copy(n).start()

    for n in range(PHASES):
        wself_copy(n).start()
    for load in loads[1:]:
        load.start()
    for n in range(2):
        cot_copy(n).start()

    @pl.loop(0, PHASES)
    def _(f):
        cache_copy(f).wait()

        @pl.loop(0, PAIRS)
        def _(i):
            arrive(f, i, 1)
            swap(f, i).start()

            @pl.when(i >= SWAP_LAG)
            def _():
                after_swap(f, i - SWAP_LAG)

            @pl.when(f == 0)
            def _():
                dequantize(i)

            @pl.when((f == 1) & (i == 0))
            def _():
                for load in loads[1:]:
                    load.wait()

            @pl.when((f == 1) & (i < PHASES))
            def _():
                begin(i)

            @pl.when((f >= 1) & (i >= 4))
            def _():
                combine_taken(f - 1, i - 4)

        @pl.loop(0, PAIRS)
        def _(i):
            arrive(f, i, 0)
            onward(f, i, 0).start()

            @pl.when(i < SWAP_LAG)
            def _():
                after_swap(f, i + PAIRS - SWAP_LAG)

            group, dz, _ = offset(i)
            combine(f, group, dz, 0)
            look[lax.rem(f, 2), i] = own[i, :, columns(f)]

            @pl.when((f >= 1) & (i < 4))
            def _():
                combine_taken(f - 1, i + 4)

            @pl.when((f >= 1) & (i == 4) & (f + 1 < PHASES))
            def _():
                cache_copy(f + 1).start()

            @pl.when((f >= 1) & (i >= 4))
            def _():
                aggregate(f - 1, i - 4)

    @pl.loop(0, PAIRS)
    def _(i):
        combine_taken(PHASES - 1, i)

    for g in range(4):
        aggregate(PHASES - 1, g)

    @pl.loop(0, PAIRS)
    def _(i):
        @pl.when(leaves(i))
        def _():
            pltpu.make_async_copy(xfer.at[0], xfer.at[0], send_sem.at[i]).wait()

    pltpu.make_async_copy(xfer, xfer, swap_out).wait()

    def cross(n):
        return pltpu.make_async_remote_copy(
            src_ref=pool.at[n, 1 - c], dst_ref=got0.at[n],
            send_sem=cross_out, recv_sem=cross_in.at[n],
            device_id=other, device_id_type=MESH,
        )

    def hop(n, h, off):
        if h == 0:
            goal = lax.rem(x + off, 4)
            src, to = xfer.at[n, pl.ds(0, 2), :, goal], (dom, goal)
        else:
            goal = lax.rem(y + off, 4)
            src, to = xfer.at[n, pl.ds(2, 2), goal], (dom_of(z, goal, c), x)
        return pltpu.make_async_remote_copy(
            src_ref=src, dst_ref=got1.at[n, h, off - 1],
            send_sem=hop_out, recv_sem=hop_in.at[n],
            device_id=to, device_id_type=MESH,
        )

    def last(n, zz, k):
        goal = lax.rem((y if zz < 2 else x) + k, 4)
        return pltpu.make_async_remote_copy(
            src_ref=sum1.at[n, zz, goal], dst_ref=got2.at[n, lax.rem(zz + 4 - z, 4) * 4 + k],
            send_sem=last_out, recv_sem=last_in.at[n],
            device_id=(dom_of(zz, goal, c), x) if zz < 2 else (dom_of(zz, y, c), goal), device_id_type=MESH,
        )

    def pair_up(n):
        cross(n).wait_recv()
        for zz in range(4):
            xfer[n, zz] = (pool[n, c, zz].astype(F32) + got0[n, zz].astype(F32)).astype(BF16)
        for off in (2, 1, 3):
            for h in range(2):
                hop(n, h, off).start()

    def spread(n):
        pltpu.make_async_copy(got1.at[n], got1.at[n], hop_in.at[n]).wait()
        for h in range(2):
            part = (xfer[n, 0:2, :, x] if h == 0 else xfer[n, 2:4, y]).astype(F32)
            for off in range(3):
                part = part + got1[n, h, off].astype(F32)
            sum1[n, 2 * h:2 * h + 2] = part.astype(BF16)
        for k in (2, 1, 3, 0):
            for zz in range(4):
                if k:
                    last(n, zz, k).start()
                else:
                    pl.when(zz != z)(last(n, zz, k).start)

    def close(n):
        came = got2.at[n, pl.ds(1, 15)]
        pltpu.make_async_copy(came, came, last_in.at[n]).wait()
        part = sum1[n, z, jnp.where(z < 2, y, x)].astype(F32)
        for j in range(1, 16):
            part = part + got2[n, j].astype(F32)
        grad_ref[:, n * WIDE:(n + 1) * WIDE] = part * factor

    def activate(n, t):
        pre = acc[t, :, n * WIDE:(n + 1) * WIDE]
        gate = jax.nn.sigmoid(pre)
        out_ref[t, :, n * WIDE:(n + 1) * WIDE] = (pre * gate).astype(BF16)
        delta[n % 2, t] = (cot[n % 2, t].astype(F32) * gate * (1.0 + pre * (1.0 - gate))).astype(BF16)

    def before(n):
        cot_copy(n).wait()

    def after(n):
        if n + 2 < PHASES:
            cot_copy(n + 2).start()

    before(0)

    @pl.loop(0, TARGETS // 4)
    def _(g):
        for q in range(4):
            activate(0, 4 * g + q)

    after(0)
    for n in range(PHASES):
        if n + 1 < PHASES:
            before(n + 1)

        @pl.loop(0, 2)
        def _(half):
            lhs = [both_t[jnp.where(half == 0, self_ref[0, t], 8 + t)] for t in range(TARGETS)]
            part = jnp.dot(
                jnp.concatenate(lhs, axis=1), delta[n % 2].reshape(TARGETS * BLOCK, WIDE), preferred_element_type=F32
            ).astype(BF16).reshape(2, 4, 2, 4, 16, WIDE)
            for core in range(2):
                pool[n, core, pl.ds(2 * half, 2)] = part[:, :, core]
            if n + 1 < PHASES:
                for q in range(8):
                    activate(n + 1, 8 * half + q)

        cross(n).start()
        if n + 1 < PHASES:
            after(n + 1)
        if n >= 1:
            pair_up(n - 1)
        if n >= 2:
            spread(n - 2)

    pair_up(PHASES - 1)
    spread(PHASES - 2)
    for n in range(PHASES - 2):
        close(n)
    spread(PHASES - 1)
    close(PHASES - 2)
    close(PHASES - 1)

    pltpu.make_async_copy(pool, pool, pass_sem).wait()
    pltpu.make_async_copy(got0, got0, cross_out).wait()
    pltpu.make_async_copy(got1, got1, hop_out).wait()
    went = got2.at[:, pl.ds(1, 15)]
    pltpu.make_async_copy(went, went, last_out).wait()


def layer(factor, send_list, near, batch, scale, own, edges, cache, w_self, w_neigh, cot):
    vmem = pl.BlockSpec(memory_space=pltpu.VMEM)
    smem = pl.BlockSpec(memory_space=pltpu.SMEM)
    hbm = pl.BlockSpec(memory_space=pl.ANY)
    dma = pltpu.SemaphoreType.DMA
    return pl.pallas_call(
        functools.partial(layer_kernel, factor),
        out_shape=(
            pltpu.VMEM((TARGETS, BLOCK, FEATS), BF16),
            pltpu.VMEM((16, FEATS), F32),
        ),
        in_specs=[smem] * 3 + [vmem] + [hbm] * 6,
        out_specs=(vmem, vmem),
        scratch_shapes=[
            pltpu.VMEM((8, BLOCK, FEATS), BF16),
            pltpu.VMEM((TARGETS, 6, BLOCK, BLOCK), BF16),
            pltpu.VMEM((FEATS, FEATS), BF16),
            pltpu.VMEM((2, 32, BLOCK, WIDE), BF16),
            pltpu.VMEM((2, TARGETS, BLOCK, WIDE), BF16),
            pltpu.VMEM((8, BLOCK, WIDE), F32),
            pltpu.VMEM((2, 40, BLOCK, WIDE), BF16),
            pltpu.VMEM((TARGETS, BLOCK, FEATS), F32),
            pltpu.VMEM((8 + TARGETS, FEATS, BLOCK), BF16),
            pltpu.VMEM((2, TARGETS, BLOCK, WIDE), BF16),
            pltpu.VMEM((PHASES, 2, 4, 4, 4, 16, WIDE), BF16),
            pltpu.VMEM((PHASES, 32) + PIECE, BF16),
            pltpu.VMEM((PHASES, 4, 4, 4, 16, WIDE), BF16),
            pltpu.VMEM((PHASES, 4, 4, 4, 16, WIDE), BF16),
            pltpu.VMEM((PHASES, 2, 3, 2, 4, 16, WIDE), BF16),
            pltpu.VMEM((PHASES, 4, 4, 16, WIDE), BF16),
            pltpu.VMEM((PHASES, 16, 16, WIDE), BF16),
            pltpu.SMEM((8,), F32),
            dma((3,)), dma((PHASES,)), dma((2,)), dma((2,)),
            dma((PAIRS,)), dma((PHASES, PAIRS, 2)), dma, dma((PHASES, PAIRS)), dma, dma((PHASES, PAIRS)),
            dma, dma((PHASES,)), dma, dma((PHASES,)), dma, dma((PHASES,)),
        ],
        compiler_params=pltpu.CompilerParams(
            collective_id=0, has_side_effects=True, vmem_limit_bytes=58 * 2**20
        ),
        name="layer",
    )(send_list, near, batch, scale, own, edges, cache, w_self, w_neigh, cot)


def on_device(
    own_values, own_scale, halo_cache, send_list, batch_ids, neighbor_blocks, edge_tiles, w_self, w_neigh, cotangent,
):
    rows = cotangent.shape[0] * lax.axis_size("dom") * lax.axis_size("rep")
    output_rows, grads = layer(
        1.0 / math.sqrt(rows), send_list, neighbor_blocks.transpose(2, 0, 1), batch_ids, own_scale.reshape(1, 8),
        own_values.reshape(8, BLOCK, FEATS), edge_tiles[0], halo_cache.reshape(32, BLOCK, FEATS),
        w_self.reshape(8, BLOCK, FEATS), w_neigh, cotangent.reshape(TARGETS, BLOCK, FEATS),
    )
    return output_rows.reshape(-1, FEATS), grads


def solution(mesh):
    placed = (
        P("dom", None), P("dom"), P("dom", None), P("dom", None), P("dom", "rep"), P("dom", "rep", None),
        P("dom", "rep", None, None, None), P(), P(), P(("dom", "rep"), None),
    )
    return jax.shard_map(
        on_device,
        mesh=mesh,
        in_specs=placed,
        out_specs=(P(("dom", "rep"), None), P(("dom", "rep"), None)),
        check_vma=False,
    )
```

```python
import functools
import math

import jax
import jax.numpy as jnp
from jax import lax
from jax.experimental import pallas as pl
from jax.experimental.pallas import tpu as pltpu
from jax.sharding import PartitionSpec as P

MOMENTUM = 0.6
MESH = pl.DeviceIdType.MESH
BLOCK = 128
FEATS = 1024
PHASES = 4
WIDE = FEATS // PHASES
PAIRS = 8
TARGETS = 16
PIECE = (2, 4, 16, WIDE)
SWAP_LAG = 1
F32 = jnp.float32
BF16 = jnp.bfloat16


def dom_of(z, y, c):
    return (z * 4 + y) * 2 + c


def columns(f):
    return pl.ds(pl.multiple_of(f * WIDE, WIDE), WIDE)


def layer_kernel(
    factor,
    send_ref, near_ref, self_ref, scale_vmem, own_hbm, edge_hbm, cache_hbm, wself_hbm, wneigh_hbm, cot_hbm,
    out_ref, grad_ref,
    own, edge, wneigh, cache, cot, base, look, acc, both_t, delta,
    pool, recv, xfer, got0, got1, sum1, got2, scale_ref,
    load_sem, wself_sem, cache_sem, cot_sem,
    send_sem, recv_sem, swap_out, swap_in, pass_sem, take_sem, cross_out, cross_in, hop_out, hop_in, last_out, last_in,
):
    dom, x = lax.axis_index("dom"), lax.axis_index("rep")
    z, y, c = dom // 8, lax.rem(dom // 2, 4), lax.rem(dom, 2)
    right, left = lax.rem(x + 1, 4), lax.rem(x + 3, 4)
    other = (dom_of(z, y, 1 - c), x)

    loads = [
        pltpu.make_async_copy(src, dst, load_sem.at[n])
        for n, (src, dst) in enumerate(((own_hbm, own), (wneigh_hbm, wneigh), (edge_hbm, edge)))
    ]

    def wself(n):
        return delta.at[n // 2, pl.ds(lax.rem(n, 2) * 8, 8)]

    def wself_copy(n):
        return pltpu.make_async_copy(wself_hbm.at[:, :, columns(n)], wself(n), wself_sem.at[n])

    def cache_copy(f):
        s = lax.rem(f, 2)
        return pltpu.make_async_copy(cache_hbm.at[:, :, columns(f)], cache.at[s], cache_sem.at[s])

    def cot_copy(n):
        return pltpu.make_async_copy(cot_hbm.at[:, :, columns(n)], cot.at[n % 2], cot_sem.at[n % 2])

    loads[0].start()

    barrier = pltpu.get_barrier_semaphore()

    @pl.loop(1, 16)
    def _(j):
        to = dom_of(lax.rem(z + j // 4, 4), lax.rem(y + lax.rem(j, 4), 4), c)
        pl.semaphore_signal(barrier, inc=1, device_id=(to, x), device_id_type=MESH)

    @pl.loop(0, 12)
    def _(j):
        to = (dom_of(lax.rem(z + j // 3, 4), y, c), lax.rem(x + 1 + lax.rem(j, 3), 4))
        pl.semaphore_signal(barrier, inc=1, device_id=to, device_id_type=MESH)

    pl.semaphore_signal(barrier, inc=1, device_id=other, device_id_type=MESH)

    def offset(i):
        group, dz = lax.rem(x + lax.rem(i, 2), 4), i // 2
        return group, dz, lax.rem(group + 4 - dz, 4)

    def slot_of(group, dz, dc):
        return group * 8 + dz * 2 + dc

    def staged(f, i, w):
        return pool.at[f, i // 4, lax.rem(i, 4), pl.ds(2 * w, 2)]

    def handed(f, i):
        return xfer.at[f, i // 2, pl.ds(2 * lax.rem(i, 2), 2)]

    def target(f, i, w):
        group, dz, _ = offset(i)
        return recv.at[f, slot_of(group, dz, 0)] if w == 0 else handed(f, i)

    def direct(f, i, w):
        _, dz, dy = offset(i)
        return pltpu.make_async_remote_copy(
            src_ref=staged(f, i, w), dst_ref=target(f, i, w),
            send_sem=send_sem.at[i], recv_sem=recv_sem.at[f, i, w],
            device_id=(dom_of(lax.rem(z + dz, 4), lax.rem(y + dy, 4), c), x), device_id_type=MESH,
        )

    def leaves(i):
        group, dz, _ = offset(i)
        return group * 4 + dz != 0

    def fill(f):
        @pl.loop(0, PAIRS)
        def _(i):
            _, dz, dy = offset(i)
            pieces = []
            for core in (c, 1 - c):
                chosen = send_ref[0, dom_of(lax.rem(z + dz, 4), lax.rem(y + dy, 4), core)]
                gain = scale_ref[chosen] * MOMENTUM
                pieces.append((own[chosen, :, columns(f)].astype(F32) * gain).astype(BF16).reshape(PIECE))

            @pl.when(leaves(i))
            def _():
                for w in range(2):
                    pool[f, i // 4, lax.rem(i, 4), pl.ds(2 * w, 2)] = pieces[w]

            @pl.when(jnp.logical_not(leaves(i)))
            def _():
                recv[f, 0] = pieces[0]
                xfer[f, i // 2, pl.ds(2 * lax.rem(i, 2), 2)] = pieces[1]

    def send(f, i, w):
        @pl.when(leaves(i))
        def _():
            direct(f, i, w).start()

    def arrive(f, i, w):
        @pl.when(leaves(i))
        def _():
            direct(f, i, w).wait_recv()

    def swap(f, i):
        group, dz, _ = offset(i)
        return pltpu.make_async_remote_copy(
            src_ref=handed(f, i), dst_ref=recv.at[f, slot_of(group, dz, 1)],
            send_sem=swap_out, recv_sem=swap_in.at[f, i],
            device_id=other, device_id_type=MESH,
        )

    def onward(f, i, dc):
        group, dz, _ = offset(i)
        slot = slot_of(group, dz, dc)
        return pltpu.make_async_remote_copy(
            src_ref=recv.at[f, slot], dst_ref=recv.at[f, slot],
            send_sem=pass_sem, recv_sem=take_sem.at[f, i],
            device_id=(dom, jnp.where(lax.rem(i, 2) == 0, right, left)), device_id_type=MESH,
        )

    def taken(f, i):
        both = recv.at[f, pl.ds(slot_of(lax.rem(x + 3 - lax.rem(i, 2), 4), i // 2, 0), 2)]
        return pltpu.make_async_copy(both, both, take_sem.at[f, i])

    def after_swap(f, i):
        swap(f, i).wait_recv()
        onward(f, i, 1).start()
        group, dz, _ = offset(i)
        combine(f, group, dz, 1)

    def dequantize(b):
        rows = (own[b].astype(F32) * scale_ref[b]).astype(BF16)
        own[b] = rows
        both_t[b] = rows.T

    def begin(n):
        wself_copy(n).wait()
        base[...] = jnp.dot(
            own[...].reshape(FEATS, FEATS), wself(n)[...].reshape(FEATS, WIDE), preferred_element_type=F32
        ).reshape(8, BLOCK, WIDE)

        @pl.loop(0, TARGETS)
        def _(t):
            acc[t, :, columns(n)] = base[self_ref[0, t]]

    def combine(f, group, dz, dc):
        dy = lax.rem(group + 4 - dz, 4)
        src = dom_of(lax.rem(z + 4 - dz, 4), lax.rem(y + 4 - dy, 4), c if dc == 0 else 1 - c)
        fresh = recv[f, slot_of(group, dz, dc)].reshape(BLOCK, WIDE).astype(F32)
        side = lax.rem(f, 2)
        look[side, 8 + src] = (fresh + (1.0 - MOMENTUM) * cache[side, src].astype(F32)).astype(BF16)

    def combine_taken(f, i):
        taken(f, i).wait()
        for dc in range(2):
            combine(f, lax.rem(x + 3 - lax.rem(i, 2), 4), i // 2, dc)

    def aggregate(f, g):
        parts = []
        for q in range(4):
            t = 4 * g + q
            coefs = jnp.concatenate([edge[t, k] for k in range(6)], axis=1)
            rows = jnp.concatenate([look[lax.rem(f, 2), near_ref[k, 0, t]] for k in range(6)], axis=0)
            part = jnp.dot(coefs, rows, preferred_element_type=F32).astype(BF16)
            both_t[8 + t, columns(f), :] = part.T
            parts.append(part)
        whole = jnp.concatenate(parts, axis=0)
        for n in range(PHASES):
            cols = slice(n * WIDE, (n + 1) * WIDE)
            more = jnp.dot(whole, wneigh[columns(f), cols], preferred_element_type=F32)
            acc[pl.ds(4 * g, 4), :, cols] += more.reshape(4, BLOCK, WIDE)

    lane = lax.broadcasted_iota(jnp.int32, (1, 8), 1)
    for b in range(8):
        scale_ref[b] = jnp.sum(jnp.where(lane == b, scale_vmem[...].astype(F32), 0.0))

    loads[0].wait()
    fill(0)
    pl.semaphore_wait(barrier, 28)
    for f in range(PHASES):
        if f:
            fill(f)
        for w in (1, 0):
            @pl.loop(0, PAIRS)
            def _(i):
                send(f, i, w)

        if f == 0:
            for n in range(2):
                cache_copy(n).start()

    for n in range(PHASES):
        wself_copy(n).start()
    for load in loads[1:]:
        load.start()
    for n in range(2):
        cot_copy(n).start()

    @pl.loop(0, PHASES)
    def _(f):
        cache_copy(f).wait()

        @pl.loop(0, PAIRS)
        def _(i):
            arrive(f, i, 1)
            swap(f, i).start()

            @pl.when(i >= SWAP_LAG)
            def _():
                after_swap(f, i - SWAP_LAG)

            @pl.when(f == 0)
            def _():
                dequantize(i)

            @pl.when((f == 1) & (i == 0))
            def _():
                for load in loads[1:]:
                    load.wait()

            @pl.when((f == 1) & (i < PHASES))
            def _():
                begin(i)

            @pl.when((f >= 1) & (i >= 4))
            def _():
                combine_taken(f - 1, i - 4)

        @pl.loop(0, PAIRS)
        def _(i):
            arrive(f, i, 0)
            onward(f, i, 0).start()

            @pl.when(i < SWAP_LAG)
            def _():
                after_swap(f, i + PAIRS - SWAP_LAG)

            group, dz, _ = offset(i)
            combine(f, group, dz, 0)
            look[lax.rem(f, 2), i] = own[i, :, columns(f)]

            @pl.when((f >= 1) & (i < 4))
            def _():
                combine_taken(f - 1, i + 4)

            @pl.when((f >= 1) & (i == 4) & (f + 1 < PHASES))
            def _():
                cache_copy(f + 1).start()

            @pl.when((f >= 1) & (i >= 4))
            def _():
                aggregate(f - 1, i - 4)

    @pl.loop(0, PAIRS)
    def _(i):
        combine_taken(PHASES - 1, i)

    def activate(n, t):
        pre = acc[t, :, n * WIDE:(n + 1) * WIDE]
        gate = jax.nn.sigmoid(pre)
        out_ref[t, :, n * WIDE:(n + 1) * WIDE] = (pre * gate).astype(BF16)
        delta[n % 2, t] = (cot[n % 2, t].astype(F32) * gate * (1.0 + pre * (1.0 - gate))).astype(BF16)

    def before(n):
        cot_copy(n).wait()

    def after(n):
        if n + 2 < PHASES:
            cot_copy(n + 2).start()

    before(0)
    for g in range(4):
        aggregate(PHASES - 1, g)
        for q in range(4):
            activate(0, 4 * g + q)

    @pl.loop(0, PAIRS)
    def _(i):
        @pl.when(leaves(i))
        def _():
            pltpu.make_async_copy(xfer.at[0], xfer.at[0], send_sem.at[i]).wait()

    pltpu.make_async_copy(xfer, xfer, swap_out).wait()

    def cross(n):
        return pltpu.make_async_remote_copy(
            src_ref=pool.at[n, 1 - c], dst_ref=got0.at[n],
            send_sem=cross_out, recv_sem=cross_in.at[n],
            device_id=other, device_id_type=MESH,
        )

    def hop(n, h, off):
        if h == 0:
            goal = lax.rem(x + off, 4)
            src, to = xfer.at[n, pl.ds(0, 2), :, goal], (dom, goal)
        else:
            goal = lax.rem(y + off, 4)
            src, to = xfer.at[n, pl.ds(2, 2), goal], (dom_of(z, goal, c), x)
        return pltpu.make_async_remote_copy(
            src_ref=src, dst_ref=got1.at[n, h, off - 1],
            send_sem=hop_out, recv_sem=hop_in.at[n],
            device_id=to, device_id_type=MESH,
        )

    def last(n, zz, k):
        goal = lax.rem((y if zz < 2 else x) + k, 4)
        return pltpu.make_async_remote_copy(
            src_ref=sum1.at[n, zz, goal], dst_ref=got2.at[n, lax.rem(zz + 4 - z, 4) * 4 + k],
            send_sem=last_out, recv_sem=last_in.at[n],
            device_id=(dom_of(zz, goal, c), x) if zz < 2 else (dom_of(zz, y, c), goal), device_id_type=MESH,
        )

    def pair_up(n):
        cross(n).wait_recv()
        for zz in range(4):
            xfer[n, zz] = (pool[n, c, zz].astype(F32) + got0[n, zz].astype(F32)).astype(BF16)
        for off in (2, 1, 3):
            for h in range(2):
                hop(n, h, off).start()

    def spread(n):
        pltpu.make_async_copy(got1.at[n], got1.at[n], hop_in.at[n]).wait()
        for h in range(2):
            part = (xfer[n, 0:2, :, x] if h == 0 else xfer[n, 2:4, y]).astype(F32)
            for off in range(3):
                part = part + got1[n, h, off].astype(F32)
            sum1[n, 2 * h:2 * h + 2] = part.astype(BF16)
        for k in (2, 1, 3, 0):
            for zz in range(4):
                if k:
                    last(n, zz, k).start()
                else:
                    pl.when(zz != z)(last(n, zz, k).start)

    def close(n):
        came = got2.at[n, pl.ds(1, 15)]
        pltpu.make_async_copy(came, came, last_in.at[n]).wait()
        part = sum1[n, z, jnp.where(z < 2, y, x)].astype(F32)
        for j in range(1, 16):
            part = part + got2[n, j].astype(F32)
        grad_ref[:, n * WIDE:(n + 1) * WIDE] = part * factor

    after(0)
    for n in range(PHASES):
        if n + 1 < PHASES:
            before(n + 1)

        @pl.loop(0, 2)
        def _(half):
            lhs = [both_t[jnp.where(half == 0, self_ref[0, t], 8 + t)] for t in range(TARGETS)]
            part = jnp.dot(
                jnp.concatenate(lhs, axis=1), delta[n % 2].reshape(TARGETS * BLOCK, WIDE), preferred_element_type=F32
            ).astype(BF16).reshape(2, 4, 2, 4, 16, WIDE)
            for core in range(2):
                pool[n, core, pl.ds(2 * half, 2)] = part[:, :, core]
            if n + 1 < PHASES:
                for q in range(8):
                    activate(n + 1, 8 * half + q)

        cross(n).start()
        if n + 1 < PHASES:
            after(n + 1)
        if n >= 1:
            pair_up(n - 1)
        if n >= 2:
            spread(n - 2)

    pair_up(PHASES - 1)
    spread(PHASES - 2)
    for n in range(PHASES - 2):
        close(n)
    spread(PHASES - 1)
    close(PHASES - 2)
    close(PHASES - 1)

    pltpu.make_async_copy(pool, pool, pass_sem).wait()
    pltpu.make_async_copy(got0, got0, cross_out).wait()
    pltpu.make_async_copy(got1, got1, hop_out).wait()
    went = got2.at[:, pl.ds(1, 15)]
    pltpu.make_async_copy(went, went, last_out).wait()


def layer(factor, send_list, near, batch, scale, own, edges, cache, w_self, w_neigh, cot):
    vmem = pl.BlockSpec(memory_space=pltpu.VMEM)
    smem = pl.BlockSpec(memory_space=pltpu.SMEM)
    hbm = pl.BlockSpec(memory_space=pl.ANY)
    dma = pltpu.SemaphoreType.DMA
    return pl.pallas_call(
        functools.partial(layer_kernel, factor),
        out_shape=(
            pltpu.VMEM((TARGETS, BLOCK, FEATS), BF16),
            pltpu.VMEM((16, FEATS), F32),
        ),
        in_specs=[smem] * 3 + [vmem] + [hbm] * 6,
        out_specs=(vmem, vmem),
        scratch_shapes=[
            pltpu.VMEM((8, BLOCK, FEATS), BF16),
            pltpu.VMEM((TARGETS, 6, BLOCK, BLOCK), BF16),
            pltpu.VMEM((FEATS, FEATS), BF16),
            pltpu.VMEM((2, 32, BLOCK, WIDE), BF16),
            pltpu.VMEM((2, TARGETS, BLOCK, WIDE), BF16),
            pltpu.VMEM((8, BLOCK, WIDE), F32),
            pltpu.VMEM((2, 40, BLOCK, WIDE), BF16),
            pltpu.VMEM((TARGETS, BLOCK, FEATS), F32),
            pltpu.VMEM((8 + TARGETS, FEATS, BLOCK), BF16),
            pltpu.VMEM((2, TARGETS, BLOCK, WIDE), BF16),
            pltpu.VMEM((PHASES, 2, 4, 4, 4, 16, WIDE), BF16),
            pltpu.VMEM((PHASES, 32) + PIECE, BF16),
            pltpu.VMEM((PHASES, 4, 4, 4, 16, WIDE), BF16),
            pltpu.VMEM((PHASES, 4, 4, 4, 16, WIDE), BF16),
            pltpu.VMEM((PHASES, 2, 3, 2, 4, 16, WIDE), BF16),
            pltpu.VMEM((PHASES, 4, 4, 16, WIDE), BF16),
            pltpu.VMEM((PHASES, 16, 16, WIDE), BF16),
            pltpu.SMEM((8,), F32),
            dma((3,)), dma((PHASES,)), dma((2,)), dma((2,)),
            dma((PAIRS,)), dma((PHASES, PAIRS, 2)), dma, dma((PHASES, PAIRS)), dma, dma((PHASES, PAIRS)),
            dma, dma((PHASES,)), dma, dma((PHASES,)), dma, dma((PHASES,)),
        ],
        compiler_params=pltpu.CompilerParams(
            collective_id=0, has_side_effects=True, vmem_limit_bytes=58 * 2**20
        ),
        name="layer",
    )(send_list, near, batch, scale, own, edges, cache, w_self, w_neigh, cot)


def on_device(
    own_values, own_scale, halo_cache, send_list, batch_ids, neighbor_blocks, edge_tiles, w_self, w_neigh, cotangent,
):
    rows = cotangent.shape[0] * lax.axis_size("dom") * lax.axis_size("rep")
    output_rows, grads = layer(
        1.0 / math.sqrt(rows), send_list, neighbor_blocks.transpose(2, 0, 1), batch_ids, own_scale.reshape(1, 8),
        own_values.reshape(8, BLOCK, FEATS), edge_tiles[0], halo_cache.reshape(32, BLOCK, FEATS),
        w_self.reshape(8, BLOCK, FEATS), w_neigh, cotangent.reshape(TARGETS, BLOCK, FEATS),
    )
    return output_rows.reshape(-1, FEATS), grads


def solution(mesh):
    placed = (
        P("dom", None), P("dom"), P("dom", None), P("dom", None), P("dom", "rep"), P("dom", "rep", None),
        P("dom", "rep", None, None, None), P(), P(), P(("dom", "rep"), None),
    )
    return jax.shard_map(
        on_device,
        mesh=mesh,
        in_specs=placed,
        out_specs=(P(("dom", "rep"), None), P(("dom", "rep"), None)),
        check_vma=False,
    )
```

```python
import functools
import math

import jax
import jax.numpy as jnp
from jax import lax
from jax.experimental import pallas as pl
from jax.experimental.pallas import tpu as pltpu
from jax.sharding import PartitionSpec as P

MOMENTUM = 0.6
MESH = pl.DeviceIdType.MESH
BLOCK = 128
FEATS = 1024
PHASES = 4
WIDE = FEATS // PHASES
PAIRS = 8
TARGETS = 16
PIECE = (2, 4, 16, WIDE)
SWAP_LAG = 1
F32 = jnp.float32
BF16 = jnp.bfloat16


def dom_of(z, y, c):
    return (z * 4 + y) * 2 + c


def columns(f):
    return pl.ds(pl.multiple_of(f * WIDE, WIDE), WIDE)


def layer_kernel(
    factor,
    send_ref, near_ref, self_ref, scale_vmem, own_hbm, edge_hbm, cache_hbm, wself_hbm, wneigh_hbm, cot_hbm,
    out_ref, grad_ref,
    own, edge, wneigh, cache, cot, base, look, acc, both_t, delta,
    extra, pool, recv, xfer, got0, got1, sum1, got2, scale_ref,
    load_sem, wself_sem, cache_sem, cot_sem,
    send_sem, recv_sem, swap_out, swap_in, pass_sem, take_sem, cross_out, cross_in, hop_out, hop_in, last_out, last_in,
):
    dom, x = lax.axis_index("dom"), lax.axis_index("rep")
    z, y, c = dom // 8, lax.rem(dom // 2, 4), lax.rem(dom, 2)
    right, left = lax.rem(x + 1, 4), lax.rem(x + 3, 4)
    other = (dom_of(z, y, 1 - c), x)

    loads = [
        pltpu.make_async_copy(src, dst, load_sem.at[n])
        for n, (src, dst) in enumerate(((own_hbm, own), (wneigh_hbm, wneigh), (edge_hbm, edge)))
    ]

    def wself(n):
        return delta.at[n // 2, pl.ds(lax.rem(n, 2) * 8, 8)]

    def wself_copy(n):
        return pltpu.make_async_copy(wself_hbm.at[:, :, columns(n)], wself(n), wself_sem.at[n])

    def cache_copy(f):
        s = lax.rem(f, 2)
        return pltpu.make_async_copy(cache_hbm.at[:, :, columns(f)], cache.at[s], cache_sem.at[s])

    def cot_copy(n):
        return pltpu.make_async_copy(cot_hbm.at[:, :, columns(n)], cot.at[n % 2], cot_sem.at[n % 2])

    loads[0].start()

    barrier = pltpu.get_barrier_semaphore()

    @pl.loop(1, 16)
    def _(j):
        to = dom_of(lax.rem(z + j // 4, 4), lax.rem(y + lax.rem(j, 4), 4), c)
        pl.semaphore_signal(barrier, inc=1, device_id=(to, x), device_id_type=MESH)

    @pl.loop(0, 12)
    def _(j):
        to = (dom_of(lax.rem(z + j // 3, 4), y, c), lax.rem(x + 1 + lax.rem(j, 3), 4))
        pl.semaphore_signal(barrier, inc=1, device_id=to, device_id_type=MESH)

    pl.semaphore_signal(barrier, inc=1, device_id=other, device_id_type=MESH)
    for k in range(2):
        source = dom_of(lax.rem(z + 1, 4), lax.rem(y + 4 - lax.rem(x + 3 + k, 4), 4), 1 - c)
        pl.semaphore_signal(barrier, inc=1, device_id=(source, x), device_id_type=MESH)

    def offset(i):
        group, dz = lax.rem(x + lax.rem(i, 2), 4), i // 2
        return group, dz, lax.rem(group + 4 - dz, 4)

    def slot_of(group, dz, dc):
        return group * 8 + dz * 2 + dc

    def staged(f, i, w):
        return pool.at[f, i // 4, lax.rem(i, 4), pl.ds(2 * w, 2)]

    def handed(f, i):
        return xfer.at[f, i // 2, pl.ds(2 * lax.rem(i, 2), 2)]

    def target(f, i, w):
        group, dz, _ = offset(i)
        return recv.at[f, slot_of(group, dz, 0)] if w == 0 else handed(f, i)

    def direct(f, i, w):
        _, dz, dy = offset(i)
        return pltpu.make_async_remote_copy(
            src_ref=staged(f, i, w), dst_ref=target(f, i, w),
            send_sem=send_sem.at[i], recv_sem=recv_sem.at[f, i, w],
            device_id=(dom_of(lax.rem(z + dz, 4), lax.rem(y + dy, 4), c), x), device_id_type=MESH,
        )

    def leaves(i):
        group, dz, _ = offset(i)
        return group * 4 + dz != 0

    def fill(f):
        @pl.loop(0, PAIRS)
        def _(i):
            _, dz, dy = offset(i)
            pieces = []
            for core in (c, 1 - c):
                chosen = send_ref[0, dom_of(lax.rem(z + dz, 4), lax.rem(y + dy, 4), core)]
                gain = scale_ref[chosen] * MOMENTUM
                pieces.append((own[chosen, :, columns(f)].astype(F32) * gain).astype(BF16).reshape(PIECE))

            @pl.when(leaves(i))
            def _():
                for w in range(2):
                    pool[f, i // 4, lax.rem(i, 4), pl.ds(2 * w, 2)] = pieces[w]

            @pl.when(jnp.logical_not(leaves(i)))
            def _():
                recv[f, 0] = pieces[0]
                xfer[f, i // 2, pl.ds(2 * lax.rem(i, 2), 2)] = pieces[1]

    def send(f, i, w):
        @pl.when(leaves(i))
        def _():
            direct(f, i, w).start()

    def arrive(f, i, w):
        @pl.when(leaves(i))
        def _():
            direct(f, i, w).wait_recv()

    def swap(f, i):
        group, dz, _ = offset(i)
        return pltpu.make_async_remote_copy(
            src_ref=handed(f, i), dst_ref=recv.at[f, slot_of(group, dz, 1)],
            send_sem=swap_out, recv_sem=swap_in.at[f, i],
            device_id=other, device_id_type=MESH,
        )

    def onward(f, i, dc):
        group, dz, _ = offset(i)
        slot = slot_of(group, dz, dc)
        return pltpu.make_async_remote_copy(
            src_ref=recv.at[f, slot], dst_ref=recv.at[f, slot],
            send_sem=pass_sem, recv_sem=take_sem.at[f, i],
            device_id=(dom, jnp.where(lax.rem(i, 2) == 0, right, left)), device_id_type=MESH,
        )

    def taken(f, i):
        both = recv.at[f, pl.ds(slot_of(lax.rem(x + 3 - lax.rem(i, 2), 4), i // 2, 0), 2)]
        return pltpu.make_async_copy(both, both, take_sem.at[f, i])

    def forward(f, i, dc):
        @pl.when((f < PHASES - 1) | (i < 6))
        def _():
            onward(f, i, dc).start()

    def straight(k, dc):
        group = lax.rem(x + 2 + k, 4)
        to = dom_of(lax.rem(z + 3, 4), lax.rem(y + lax.rem(group + 1, 4), 4), c if dc == 0 else 1 - c)
        return to, pltpu.make_async_remote_copy(
            src_ref=extra.at[k, dc], dst_ref=recv.at[PHASES - 1, slot_of(group, 3, dc)],
            send_sem=pass_sem, recv_sem=take_sem.at[PHASES - 1, 7 - k],
            device_id=(to, x), device_id_type=MESH,
        )

    def send_straight():
        for k in range(2):
            for dc in range(2):
                to, copy = straight(k, dc)
                chosen = send_ref[0, to]
                rows = own[chosen, :, (PHASES - 1) * WIDE:].astype(F32) * (scale_ref[chosen] * MOMENTUM)
                extra[k, dc] = rows.astype(BF16).reshape(PIECE)
                copy.start()

    def after_swap(f, i):
        swap(f, i).wait_recv()
        forward(f, i, 1)
        group, dz, _ = offset(i)
        combine(f, group, dz, 1)

    def dequantize(b):
        rows = (own[b].astype(F32) * scale_ref[b]).astype(BF16)
        own[b] = rows
        both_t[b] = rows.T

    def begin(n):
        wself_copy(n).wait()
        base[...] = jnp.dot(
            own[...].reshape(FEATS, FEATS), wself(n)[...].reshape(FEATS, WIDE), preferred_element_type=F32
        ).reshape(8, BLOCK, WIDE)

        @pl.loop(0, TARGETS)
        def _(t):
            acc[t, :, columns(n)] = base[self_ref[0, t]]

    def combine(f, group, dz, dc):
        dy = lax.rem(group + 4 - dz, 4)
        src = dom_of(lax.rem(z + 4 - dz, 4), lax.rem(y + 4 - dy, 4), c if dc == 0 else 1 - c)
        fresh = recv[f, slot_of(group, dz, dc)].reshape(BLOCK, WIDE).astype(F32)
        side = lax.rem(f, 2)
        look[side, 8 + src] = (fresh + (1.0 - MOMENTUM) * cache[side, src].astype(F32)).astype(BF16)

    def combine_taken(f, i):
        taken(f, i).wait()
        for dc in range(2):
            combine(f, lax.rem(x + 3 - lax.rem(i, 2), 4), i // 2, dc)

    def aggregate(f, g):
        parts = []
        for q in range(4):
            t = 4 * g + q
            coefs = jnp.concatenate([edge[t, k] for k in range(6)], axis=1)
            rows = jnp.concatenate([look[lax.rem(f, 2), near_ref[k, 0, t]] for k in range(6)], axis=0)
            part = jnp.dot(coefs, rows, preferred_element_type=F32).astype(BF16)
            both_t[8 + t, columns(f), :] = part.T
            parts.append(part)
        whole = jnp.concatenate(parts, axis=0)
        for n in range(PHASES):
            cols = slice(n * WIDE, (n + 1) * WIDE)
            more = jnp.dot(whole, wneigh[columns(f), cols], preferred_element_type=F32)
            acc[pl.ds(4 * g, 4), :, cols] += more.reshape(4, BLOCK, WIDE)

    lane = lax.broadcasted_iota(jnp.int32, (1, 8), 1)
    for b in range(8):
        scale_ref[b] = jnp.sum(jnp.where(lane == b, scale_vmem[...].astype(F32), 0.0))

    loads[0].wait()
    fill(0)
    pl.semaphore_wait(barrier, 30)
    for f in range(PHASES):
        if f:
            fill(f)
        for w in (1, 0):
            @pl.loop(0, PAIRS)
            def _(i):
                send(f, i, w)

        if f == 0:
            for n in range(2):
                cache_copy(n).start()

    send_straight()
    for n in range(PHASES):
        wself_copy(n).start()
    for load in loads[1:]:
        load.start()
    for n in range(2):
        cot_copy(n).start()

    @pl.loop(0, PHASES)
    def _(f):
        cache_copy(f).wait()

        @pl.loop(0, PAIRS)
        def _(i):
            arrive(f, i, 1)
            swap(f, i).start()

            @pl.when(i >= SWAP_LAG)
            def _():
                after_swap(f, i - SWAP_LAG)

            @pl.when(f == 0)
            def _():
                dequantize(i)

            @pl.when((f == 1) & (i == 0))
            def _():
                for load in loads[1:]:
                    load.wait()

            @pl.when((f == 1) & (i < PHASES))
            def _():
                begin(i)

            @pl.when((f >= 1) & (i >= 4))
            def _():
                combine_taken(f - 1, i - 4)

        @pl.loop(0, PAIRS)
        def _(i):
            arrive(f, i, 0)
            forward(f, i, 0)

            @pl.when(i < SWAP_LAG)
            def _():
                after_swap(f, i + PAIRS - SWAP_LAG)

            group, dz, _ = offset(i)
            combine(f, group, dz, 0)
            look[lax.rem(f, 2), i] = own[i, :, columns(f)]

            @pl.when((f >= 1) & (i < 4))
            def _():
                combine_taken(f - 1, i + 4)

            @pl.when((f >= 1) & (i == 4) & (f + 1 < PHASES))
            def _():
                cache_copy(f + 1).start()

            @pl.when((f >= 1) & (i >= 4))
            def _():
                aggregate(f - 1, i - 4)

    @pl.loop(0, PAIRS)
    def _(i):
        combine_taken(PHASES - 1, i)

    def activate(n, t):
        pre = acc[t, :, n * WIDE:(n + 1) * WIDE]
        gate = jax.nn.sigmoid(pre)
        out_ref[t, :, n * WIDE:(n + 1) * WIDE] = (pre * gate).astype(BF16)
        delta[n % 2, t] = (cot[n % 2, t].astype(F32) * gate * (1.0 + pre * (1.0 - gate))).astype(BF16)

    def before(n):
        cot_copy(n).wait()

    def after(n):
        if n + 2 < PHASES:
            cot_copy(n + 2).start()

    before(0)
    for g in range(4):
        aggregate(PHASES - 1, g)
        for q in range(4):
            activate(0, 4 * g + q)

    @pl.loop(0, PAIRS)
    def _(i):
        @pl.when(leaves(i))
        def _():
            pltpu.make_async_copy(xfer.at[0], xfer.at[0], send_sem.at[i]).wait()

    pltpu.make_async_copy(xfer, xfer, swap_out).wait()

    def cross(n):
        return pltpu.make_async_remote_copy(
            src_ref=pool.at[n, 1 - c], dst_ref=got0.at[n],
            send_sem=cross_out, recv_sem=cross_in.at[n],
            device_id=other, device_id_type=MESH,
        )

    def hop(n, h, off):
        if h == 0:
            goal = lax.rem(x + off, 4)
            src, to = xfer.at[n, pl.ds(0, 2), :, goal], (dom, goal)
        else:
            goal = lax.rem(y + off, 4)
            src, to = xfer.at[n, pl.ds(2, 2), goal], (dom_of(z, goal, c), x)
        return pltpu.make_async_remote_copy(
            src_ref=src, dst_ref=got1.at[n, h, off - 1],
            send_sem=hop_out, recv_sem=hop_in.at[n],
            device_id=to, device_id_type=MESH,
        )

    def last(n, zz, k):
        goal = lax.rem((y if zz < 2 else x) + k, 4)
        return pltpu.make_async_remote_copy(
            src_ref=sum1.at[n, zz, goal], dst_ref=got2.at[n, lax.rem(zz + 4 - z, 4) * 4 + k],
            send_sem=last_out, recv_sem=last_in.at[n],
            device_id=(dom_of(zz, goal, c), x) if zz < 2 else (dom_of(zz, y, c), goal), device_id_type=MESH,
        )

    def pair_up(n):
        cross(n).wait_recv()
        for zz in range(4):
            xfer[n, zz] = (pool[n, c, zz].astype(F32) + got0[n, zz].astype(F32)).astype(BF16)
        for off in (2, 1, 3):
            for h in range(2):
                hop(n, h, off).start()

    def spread(n):
        pltpu.make_async_copy(got1.at[n], got1.at[n], hop_in.at[n]).wait()
        for h in range(2):
            part = (xfer[n, 0:2, :, x] if h == 0 else xfer[n, 2:4, y]).astype(F32)
            for off in range(3):
                part = part + got1[n, h, off].astype(F32)
            sum1[n, 2 * h:2 * h + 2] = part.astype(BF16)
        for k in (2, 1, 3, 0):
            for zz in range(4):
                if k:
                    last(n, zz, k).start()
                else:
                    pl.when(zz != z)(last(n, zz, k).start)

    def close(n):
        came = got2.at[n, pl.ds(1, 15)]
        pltpu.make_async_copy(came, came, last_in.at[n]).wait()
        part = sum1[n, z, jnp.where(z < 2, y, x)].astype(F32)
        for j in range(1, 16):
            part = part + got2[n, j].astype(F32)
        grad_ref[:, n * WIDE:(n + 1) * WIDE] = part * factor

    after(0)
    for n in range(PHASES):
        if n + 1 < PHASES:
            before(n + 1)

        @pl.loop(0, 2)
        def _(half):
            lhs = [both_t[jnp.where(half == 0, self_ref[0, t], 8 + t)] for t in range(TARGETS)]
            part = jnp.dot(
                jnp.concatenate(lhs, axis=1), delta[n % 2].reshape(TARGETS * BLOCK, WIDE), preferred_element_type=F32
            ).astype(BF16).reshape(2, 4, 2, 4, 16, WIDE)
            for core in range(2):
                pool[n, core, pl.ds(2 * half, 2)] = part[:, :, core]
            if n + 1 < PHASES:
                for q in range(8):
                    activate(n + 1, 8 * half + q)

        cross(n).start()
        if n + 1 < PHASES:
            after(n + 1)
        if n >= 1:
            pair_up(n - 1)
        if n >= 2:
            spread(n - 2)

    pair_up(PHASES - 1)
    spread(PHASES - 2)
    for n in range(PHASES - 2):
        close(n)
    spread(PHASES - 1)
    close(PHASES - 2)
    close(PHASES - 1)

    pltpu.make_async_copy(pool, pool, pass_sem).wait()
    pltpu.make_async_copy(got0, got0, cross_out).wait()
    pltpu.make_async_copy(got1, got1, hop_out).wait()
    went = got2.at[:, pl.ds(1, 15)]
    pltpu.make_async_copy(went, went, last_out).wait()


def layer(factor, send_list, near, batch, scale, own, edges, cache, w_self, w_neigh, cot):
    vmem = pl.BlockSpec(memory_space=pltpu.VMEM)
    smem = pl.BlockSpec(memory_space=pltpu.SMEM)
    hbm = pl.BlockSpec(memory_space=pl.ANY)
    dma = pltpu.SemaphoreType.DMA
    return pl.pallas_call(
        functools.partial(layer_kernel, factor),
        out_shape=(
            pltpu.VMEM((TARGETS, BLOCK, FEATS), BF16),
            pltpu.VMEM((16, FEATS), F32),
        ),
        in_specs=[smem] * 3 + [vmem] + [hbm] * 6,
        out_specs=(vmem, vmem),
        scratch_shapes=[
            pltpu.VMEM((8, BLOCK, FEATS), BF16),
            pltpu.VMEM((TARGETS, 6, BLOCK, BLOCK), BF16),
            pltpu.VMEM((FEATS, FEATS), BF16),
            pltpu.VMEM((2, 32, BLOCK, WIDE), BF16),
            pltpu.VMEM((2, TARGETS, BLOCK, WIDE), BF16),
            pltpu.VMEM((8, BLOCK, WIDE), F32),
            pltpu.VMEM((2, 40, BLOCK, WIDE), BF16),
            pltpu.VMEM((TARGETS, BLOCK, FEATS), F32),
            pltpu.VMEM((8 + TARGETS, FEATS, BLOCK), BF16),
            pltpu.VMEM((2, TARGETS, BLOCK, WIDE), BF16),
            pltpu.VMEM((2, 2) + PIECE, BF16),
            pltpu.VMEM((PHASES, 2, 4, 4, 4, 16, WIDE), BF16),
            pltpu.VMEM((PHASES, 32) + PIECE, BF16),
            pltpu.VMEM((PHASES, 4, 4, 4, 16, WIDE), BF16),
            pltpu.VMEM((PHASES, 4, 4, 4, 16, WIDE), BF16),
            pltpu.VMEM((PHASES, 2, 3, 2, 4, 16, WIDE), BF16),
            pltpu.VMEM((PHASES, 4, 4, 16, WIDE), BF16),
            pltpu.VMEM((PHASES, 16, 16, WIDE), BF16),
            pltpu.SMEM((8,), F32),
            dma((3,)), dma((PHASES,)), dma((2,)), dma((2,)),
            dma((PAIRS,)), dma((PHASES, PAIRS, 2)), dma, dma((PHASES, PAIRS)), dma, dma((PHASES, PAIRS)),
            dma, dma((PHASES,)), dma, dma((PHASES,)), dma, dma((PHASES,)),
        ],
        compiler_params=pltpu.CompilerParams(
            collective_id=0, has_side_effects=True, vmem_limit_bytes=58 * 2**20
        ),
        name="layer",
    )(send_list, near, batch, scale, own, edges, cache, w_self, w_neigh, cot)


def on_device(
    own_values, own_scale, halo_cache, send_list, batch_ids, neighbor_blocks, edge_tiles, w_self, w_neigh, cotangent,
):
    rows = cotangent.shape[0] * lax.axis_size("dom") * lax.axis_size("rep")
    output_rows, grads = layer(
        1.0 / math.sqrt(rows), send_list, neighbor_blocks.transpose(2, 0, 1), batch_ids, own_scale.reshape(1, 8),
        own_values.reshape(8, BLOCK, FEATS), edge_tiles[0], halo_cache.reshape(32, BLOCK, FEATS),
        w_self.reshape(8, BLOCK, FEATS), w_neigh, cotangent.reshape(TARGETS, BLOCK, FEATS),
    )
    return output_rows.reshape(-1, FEATS), grads


def solution(mesh):
    placed = (
        P("dom", None), P("dom"), P("dom", None), P("dom", None), P("dom", "rep"), P("dom", "rep", None),
        P("dom", "rep", None, None, None), P(), P(), P(("dom", "rep"), None),
    )
    return jax.shard_map(
        on_device,
        mesh=mesh,
        in_specs=placed,
        out_specs=(P(("dom", "rep"), None), P(("dom", "rep"), None)),
        check_vma=False,
    )
```
